768 devices in a mesh: wide: 64 (over y, x, core), narrow: 12 (over z).
Axes of the slice: x: 4, y: 8, z: 12, core: 2. Of those that a mesh axis runs over, the one named last changes fastest.
Arguments:
- features: bfloat16 [393216, 256], P(('wide', 'narrow')), may hold values from -6 to 6
- upstream: bfloat16 [393216, 256], P(('wide', 'narrow')), may hold values from -6 to 6
- visit_counts: bfloat16 [1179648, 512], P(('wide', 'narrow')), may hold values from 0 to 8, as said below
- target_rows: int32 [768, 1536], P(('wide', 'narrow')), may hold values from 0 to 512, as said below
- message_weight: bfloat16 [2, 256, 256], replicated, may hold values from -0.375 to 0.375
- message_offset: float32 [2, 256], replicated, may hold values from -3 to 3
- self_weight: bfloat16 [2, 256, 256], replicated, may hold values from -0.375 to 0.375
- neighbor_weight: bfloat16 [2, 256, 256], replicated, may hold values from -0.375 to 0.375
- update_offset: float32 [2, 256], replicated, may hold values from -3 to 3
Outputs:
- embedding: bfloat16 [393216, 256], P(('wide', 'narrow'))
- input_gradient: float32 [393216, 256], P(('wide', 'narrow'))
- message_gradient: float32 [2, 256, 256], replicated
- offset_gradient: float32 [2, 256], replicated
- self_gradient: float32 [2, 256, 256], replicated
- neighbor_gradient: float32 [2, 256, 256], replicated
- update_gradient: float32 [2, 256], replicated
The draws below stay inside these ranges and needn't reach their ends.
Inputs may be any that keep to these rules, and one draw needn't show every extreme that they name: `visit_counts`: every entry is a whole number. Row s * 1536 + r * 2 + c is zero exactly where target_rows[r, s * 2 + c] is 512, and has a positive count otherwise. `target_rows`: in every draw some device receives a live row in every one of its 1536 positions; live rows never target the last 64 local nodes.
All inputs are finite; a program needn't handle non-finite values.
Results may differ from the reference program's by a relative error of at most 0.0075.
Values may be sent and summed in bfloat16 or wider, within the bound.
A program may use at most 32 MiB of HBM per device.

```python
import jax
import jax.numpy as jnp
from jax import lax

F = 256
ROWS = 512
CAP = 2
LAYERS = 2
SLOTS = 1536
NODES = 393216
N_WIDE = 64
N_NARROW = 12


def live_slots(key):
    hot_key, base_key, pick_key = jax.random.split(jax.random.fold_in(key, 101), 3)
    devices = NODES // ROWS
    base = jax.random.randint(base_key, (devices, devices, CAP), 0, 2)
    hot = jax.random.randint(hot_key, (devices,), 0, 4) == 0
    chosen = jax.random.randint(pick_key, (), 0, devices)
    hot = hot | (jnp.arange(devices) == chosen)
    return jnp.where(hot[None, :, None], 1, base)


def draw_visit_counts(key, part):
    live = live_slots(key)
    key = jax.random.fold_in(key, 3)
    value_key, keep_key, column_key = jax.random.split(key, 3)
    shape = (NODES // ROWS * SLOTS, ROWS)
    values = jax.random.randint(value_key, shape, 1, 9)
    keep = jax.random.randint(keep_key, shape, 0, 32) == 0
    column = jax.random.randint(column_key, (shape[0], 1), 0, ROWS)
    counts = jnp.where(keep | (jnp.arange(ROWS)[None, :] == column), values, 0)
    counts = counts * live.reshape(-1, 1)
    return counts.astype(jnp.float32).astype(jnp.bfloat16)


def draw_target_rows(key, part):
    live = live_slots(key)
    key = jax.random.fold_in(key, 5)
    devices = NODES // ROWS
    chosen_rows = jax.random.randint(key, (devices, devices, CAP), 0, ROWS - ROWS // 8)
    live_turned = jnp.transpose(live, (1, 0, 2))
    return jnp.where(live_turned == 1, chosen_rows, ROWS).reshape(devices, SLOTS)


def levels(own_key, dims, cuts, smallest, largest):
    factor_of = 1.0
    for dim, blocks in cuts:
        steps = jax.random.uniform(jax.random.fold_in(jax.random.fold_in(own_key, 6), dim), (blocks,), jnp.float32, smallest / len(cuts), largest / len(cuts))
        factor_of = factor_of * jnp.repeat(jnp.exp(steps), dims[dim] // blocks).reshape((-1,) + (1,) * (len(dims) - 1 - dim))
    return factor_of


def gaussian(key, dims, scale, limit, cuts=(), kind=jnp.bfloat16):
    drawn = scale * jax.random.normal(key, dims, jnp.float32)
    if cuts:
        drawn = drawn * levels(key, dims, cuts, -0.22, 0.18)
    return jnp.clip(drawn, -limit, limit).astype(kind)


def setup_inputs(seed: int = 0) -> dict:
    seeds = jax.random.split(jax.random.key(seed), 10)
    features = gaussian(seeds[0], (NODES, F), 1.0, 6.0, ((0, 768),))
    upstream = gaussian(seeds[1], (NODES, F), 1.0, 6.0, ((0, 768),))
    visit_counts = draw_visit_counts(jax.random.fold_in(seeds[9], 71), 0)
    target_rows = draw_target_rows(jax.random.fold_in(seeds[9], 71), 0)
    message_weight = gaussian(seeds[4], (LAYERS, F, F), F ** -0.5, 0.375)
    message_offset = gaussian(seeds[5], (LAYERS, F), 0.5, 3.0, (), jnp.float32)
    self_weight = gaussian(seeds[6], (LAYERS, F, F), F ** -0.5, 0.375)
    neighbor_weight = gaussian(seeds[7], (LAYERS, F, F), F ** -0.5, 0.375)
    update_offset = gaussian(seeds[8], (LAYERS, F), 0.5, 3.0, (), jnp.float32)
    return dict(features=features, upstream=upstream, visit_counts=visit_counts, target_rows=target_rows, message_weight=message_weight, message_offset=message_offset, self_weight=self_weight, neighbor_weight=neighbor_weight, update_offset=update_offset)


epsilon = 1e-05

def silu_slope(value):
    sigma = jax.nn.sigmoid(value)
    return sigma * (1.0 + value * (1.0 - sigma))

def normalize(update_pre):
    activated = jax.nn.silu(update_pre)
    scaling = lax.rsqrt(lax.optimization_barrier(jnp.mean(activated * activated, axis=-1, keepdims=True)) + epsilon)
    return (activated, scaling)

def norm_backward(upward, update_pre):
    activated, scaling = normalize(update_pre)
    inner = lax.optimization_barrier(jnp.mean(upward * activated, axis=-1, keepdims=True))
    slope = scaling * upward - activated * (scaling * scaling * scaling) * inner
    return slope * silu_slope(update_pre)

def swap_slots(grid, devices):
    rest = grid.shape[2:]
    shaped = grid.reshape((devices, devices, CAP) + rest)
    return jnp.swapaxes(shaped, 0, 1).reshape((devices, SLOTS) + rest)

def pool_rows(pair):
    return jax.ops.segment_sum(pair[0].astype(jnp.float32), pair[1], num_segments=ROWS + 1)[:ROWS]

def reference(features, upstream, visit_counts, target_rows, message_weight, message_offset, self_weight, neighbor_weight, update_offset):
    devices = N_WIDE * N_NARROW
    counts_grid = visit_counts.reshape(devices, SLOTS, ROWS)
    totals = lax.optimization_barrier(jnp.sum(counts_grid, axis=2, dtype=jnp.float32)).astype(jnp.bfloat16)
    arrived_totals = swap_slots(totals, devices)
    weight_sum = lax.map(pool_rows, (arrived_totals, target_rows))
    divisor = jnp.maximum(weight_sum, 1.0).reshape(NODES, 1)
    states = features
    saved = []
    for layer in range(LAYERS):
        message_pre = jnp.dot(states, message_weight[layer], preferred_element_type=jnp.float32) + message_offset[layer]
        messages = jax.nn.silu(message_pre).astype(jnp.bfloat16)
        partial_rows = lax.map(lambda pair: jnp.dot(pair[0], pair[1], preferred_element_type=jnp.float32).astype(jnp.bfloat16), (counts_grid, messages.reshape(devices, ROWS, F)))
        arrived = swap_slots(partial_rows, devices)
        gathered = lax.map(pool_rows, (arrived, target_rows)).reshape(NODES, F)
        neighbor_mean = (gathered / divisor).astype(jnp.bfloat16)
        update_pre = jnp.dot(states, self_weight[layer], preferred_element_type=jnp.float32) + jnp.dot(neighbor_mean, neighbor_weight[layer], preferred_element_type=jnp.float32) + update_offset[layer]
        activated, scaling = normalize(update_pre)
        saved.append((states, message_pre, neighbor_mean, update_pre))
        states = (activated * scaling).astype(jnp.bfloat16)
    embedding = states
    upward = upstream.astype(jnp.float32)
    grads = [None] * LAYERS
    for layer in reversed(range(LAYERS)):
        states_in, message_pre, neighbor_mean, update_pre = saved[layer]
        slope = norm_backward(upward, update_pre)
        slope_b = slope.astype(jnp.bfloat16)
        self_grad = jnp.dot(states_in.T, slope_b, preferred_element_type=jnp.float32)
        neighbor_grad = jnp.dot(neighbor_mean.T, slope_b, preferred_element_type=jnp.float32)
        update_grad = lax.optimization_barrier(jnp.sum(slope, axis=0))
        lower = jnp.dot(slope_b, self_weight[layer].T, preferred_element_type=jnp.float32)
        mean_slope = jnp.dot(slope_b, neighbor_weight[layer].T, preferred_element_type=jnp.float32)
        spread = (mean_slope / divisor).astype(jnp.bfloat16).reshape(devices, ROWS, F)
        padded = jnp.concatenate([spread, jnp.zeros((devices, 1, F), jnp.bfloat16)], axis=1)
        sent_back = lax.map(lambda pair: pair[0][pair[1]], (padded, target_rows))
        returned = swap_slots(sent_back, devices)
        message_slope = lax.map(lambda pair: jnp.dot(pair[0].T, pair[1], preferred_element_type=jnp.float32), (counts_grid, returned)).reshape(NODES, F)
        pre_slope = message_slope * silu_slope(message_pre)
        pre_b = pre_slope.astype(jnp.bfloat16)
        message_grad = jnp.dot(states_in.T, pre_b, preferred_element_type=jnp.float32)
        offset_grad = lax.optimization_barrier(jnp.sum(pre_slope, axis=0))
        upward = lower + jnp.dot(pre_b, message_weight[layer].T, preferred_element_type=jnp.float32)
        grads[layer] = (message_grad, offset_grad, self_grad, neighbor_grad, update_grad)
    return (embedding, upward, jnp.stack([entry[0] for entry in grads]), jnp.stack([entry[1] for entry in grads]), jnp.stack([entry[2] for entry in grads]), jnp.stack([entry[3] for entry in grads]), jnp.stack([entry[4] for entry in grads]))
```

```python
import functools

import jax
import jax.numpy as jnp
from jax import lax
from jax.experimental import pallas as pl
from jax.experimental.pallas import tpu as pltpu
from jax.sharding import PartitionSpec as P

F = 256
H = 128
NX = 4
NC = 2
GROUP = NX * NC
EPS = 1e-05
BF = jnp.bfloat16
F32 = jnp.float32
MESH = pl.DeviceIdType.MESH


def sigmoid(v):
    return 1.0 / (1.0 + jnp.exp(-v))


def silu_slope(v):
    sigma = sigmoid(v)
    return sigma * (1.0 + v * (1.0 - sigma))


def dot(a, b):
    return jnp.dot(a, b, preferred_element_type=F32)


def dot_nt(a, b):
    return lax.dot_general(a, b, (((1,), (1,)), ((), ())), preferred_element_type=F32)


def dot_tn(a, b):
    return lax.dot_general(a, b, (((0,), (0,)), ((), ())), preferred_element_type=F32)


def iota(shape, dim):
    return lax.broadcasted_iota(jnp.int32, shape, dim)


def pair_permutation(blocks):
    n = 16 * blocks
    out = iota((n, n), 0)
    source = ((out // 2) % 8) * (2 * blocks) + (out // 16) * 2 + out % 2
    return jnp.where(iota((n, n), 1) == source, 1.0, 0.0).astype(BF)


def alternate(t, n):
    s = (t + 1) // 2
    return lax.rem(s + (1 - lax.rem(t, 2)) * (n - 2 * s), n)


def kernel(
    NW, NZ, R,
    feat, ups, cnt, t_n, t_t, t_y, wm, bm, ws, wn, bu,
    emb, ing, gm, go, gs, gn, gu,
    ct, cnt_n, cnt_t, sel_n, sel_t, selt_n, selt_t, m1, m2,
    pre, upre, st, nm, base, low, div,
    sa, za, ma, xa, sb, xb, mb, zb,
    xs, xr, ys, yr,
    g1s, g1r, g1a, g1b, g1c, g1d, g1e, g1f, g1g,
    g2s, g2r, g2a, g2b, g2c, g2d, g2e, g2f, g2g,
    ssem, rsem,
):
    NP = NW // NC
    NY = NP // NX
    B = NC * NZ
    PR, BR = 2 * B, 2 * NP
    S = NP * PR
    wide = lax.axis_index("wide")
    z = lax.axis_index("narrow")
    p, c = wide // NC, lax.rem(wide, NC)
    y, x = p // NX, lax.rem(p, NX)
    q = lax.rem(wide, GROUP)
    b = c * NZ + z

    def plane_peer(d):
        dy = alternate(d // NX, NY)
        yy, xx = lax.rem(y + dy, NY), lax.rem(x + lax.rem(d, NX), NX)
        pp = yy * NX + xx
        return pp, (pp * NC + c, z)

    def column_peer(j):
        dz = alternate(j // 2, NZ)
        cc, zz = lax.rem(c + lax.rem(j, 2), NC), lax.rem(z + dz, NZ)
        return cc * NZ + zz, (p * NC + cc, zz)

    def group_peer(j):
        qq = lax.rem(q + j, GROUP)
        return qq, (y * GROUP + qq, z)

    def row_peer(j):
        yy = lax.rem(y + j, NY)
        return yy, (yy * GROUP + q, z)

    def ring_peer(j):
        zz = lax.rem(z + j, NZ)
        return zz, (wide, zz)

    def send(src, dst, slot, target):
        pltpu.make_async_remote_copy(
            src_ref=src, dst_ref=dst, send_sem=ssem.at[slot], recv_sem=rsem.at[slot],
            device_id=target, device_id_type=MESH,
        ).start()

    def scatter(src, dst, slot, mine, peer, n):
        def step(i, _):
            theirs, target = peer(n - i)
            send(src.at[theirs], dst.at[mine], slot, target)
            return _
        lax.fori_loop(1, n, step, 0)
        dst[pl.ds(mine, 1)] = src[pl.ds(mine, 1)]

    def spread_out(src, dst, slot, mine, peer, n):
        def step(i, _):
            send(src, dst.at[mine], slot, peer(n - i)[1])
            return _
        lax.fori_loop(1, n, step, 0)
        dst[pl.ds(mine, 1)] = src[...][None]

    def await_bytes(ref, sem):
        pltpu.make_async_copy(ref, ref, sem).wait()

    def arrived(dst, slot):
        await_bytes(dst.at[pl.ds(0, dst.shape[0] - 1)], rsem.at[slot])

    barrier = pltpu.get_barrier_semaphore()

    def greet(peer, first, last):
        def step(i, _):
            pl.semaphore_signal(barrier, inc=1, device_id=peer(i)[1], device_id_type=MESH)
            return _
        lax.fori_loop(first, last, step, 0)

    greet(plane_peer, 1, NP)
    greet(column_peer, 1, B)
    greet(lambda i: (i, ((y * NX + lax.rem(x + i, NX)) * NC + (1 - c), z)), 1, NX)

    def to_t_order(src, dst, width):
        for o in range(NP // 8):
            got = dot(m1[...], src[o * 8 * PR:(o + 1) * 8 * PR, :]).astype(BF)
            got = got.reshape(B, 16, width)
            for i in range(B):
                dst[i * BR + o * 16:i * BR + (o + 1) * 16, :] = got[i]

    def shuffle_b(i):
        for o in range(NP // 8):
            got = dot(m1[...], xb[i, o * 8:(o + 1) * 8].reshape(8 * PR, H)).astype(BF)
            mb[i, :, o * 16:(o + 1) * 16, :] = got.reshape(B, 16, H)

    def shuffle_a(i):
        for o in range(B // 8):
            got = dot(m2[...], za[i, o * 8:(o + 1) * 8].reshape(8 * BR, H)).astype(BF)
            ma[i, :, o * 16:(o + 1) * 16, :] = got.reshape(NP, 16, H)

    def fill_a(i, left, right):
        n = max(1, B // 6)
        rows = S // n
        for k in range(n):
            got = dot(left[k * rows:(k + 1) * rows, :], right).astype(BF)
            sa[i, k * (B // n):(k + 1) * (B // n)] = got.reshape(B // n, BR, H)

    def fill_b(i, left, right):
        n = NP // 8
        rows = S // n
        for k in range(n):
            got = dot(left[k * rows:(k + 1) * rows, :], right).astype(BF)
            sb[i, k * 8:(k + 1) * 8] = got.reshape(8, PR, H)

    def first_a(i):
        scatter(sa.at[i], za.at[i], 4 * i, b, column_peer, B)

    def first_b(i):
        scatter(sb.at[i], xb.at[i], 4 * i + 1, p, plane_peer, NP)

    def second_b(i):
        arrived(xb.at[i], 4 * i + 1)
        shuffle_b(i)
        scatter(mb.at[i], zb.at[i], 4 * i + 2, b, column_peer, B)

    def second_a(i):
        arrived(za.at[i], 4 * i)
        shuffle_a(i)
        scatter(ma.at[i], xa.at[i], 4 * i + 3, p, plane_peer, NP)

    def final_a(i):
        arrived(xa.at[i], 4 * i + 3)
        return xa[i].reshape(S, H)

    def final_b(i):
        arrived(zb.at[i], 4 * i + 2)
        return zb[i].reshape(S, H)

    def place(buf, matrix, value):
        g = value.astype(BF)
        for k in range(GROUP):
            for h in range(2):
                buf[k, matrix * 64 + h * 32:matrix * 64 + (h + 1) * 32, :] = (
                    g[k * 32:(k + 1) * 32, h * H:(h + 1) * H])

    def place_vectors(buf, rows, vectors):
        tile = jnp.zeros((16, H), F32)
        line = iota((16, H), 0)
        for v, vec in enumerate(vectors):
            for h in range(2):
                tile = jnp.where(line == 2 * v + h, vec[:, h * H:(h + 1) * H], tile)
        for k in range(GROUP):
            buf[k, rows:rows + 16, :] = tile.astype(BF)

    def reduce_1(bufs, slot):
        scatter(bufs[0], bufs[1], slot, q, group_peer, GROUP)

    def reduce_2(bufs, slot):
        s, r, a = bufs[:3]
        arrived(r, slot)
        rows = s.shape[1] - 16
        piece = rows // NY
        total = r[0].astype(F32)
        for k in range(1, GROUP):
            total = total + r[k].astype(F32)
        for k in range(NY):
            a[k, 0:piece, :] = total[k * piece:(k + 1) * piece]
            a[k, piece:piece + 8, :] = total[rows:rows + 8]
        scatter(a, bufs[3], slot + 1, y, row_peer, NY)

    def reduce_3(bufs, slot):
        r, s = bufs[3], bufs[4]
        arrived(r, slot + 1)
        total = r[0]
        for k in range(1, NY):
            total = total + r[k]
        s[...] = total
        spread_out(s, bufs[5], slot + 2, z, ring_peer, NZ)

    def reduce_4(bufs, slot):
        r, s = bufs[5], bufs[6]
        arrived(r, slot + 2)
        total = r[0]
        for k in range(1, NZ):
            total = total + r[k]
        s[...] = total
        piece = s.shape[0] - 8
        src, dst = s.at[pl.ds(0, piece)], bufs[7]

        def step(i, _):
            send(src, dst.at[y], slot + 3, row_peer(NY - i)[1])
            return _
        lax.fori_loop(1, NY, step, 0)
        dst[pl.ds(y, 1)] = s[0:piece][None]

    def reduce_5(bufs, slot):
        r, out = bufs[7], bufs[8]
        arrived(r, slot + 3)
        rows = out.shape[1]
        out[pl.ds(q, 1)] = r[...].reshape(1, rows, H).astype(BF)

        def step(i, _):
            send(out.at[q], out.at[q], slot + 4, group_peer(GROUP - i)[1])
            return _
        lax.fori_loop(1, GROUP, step, 0)

    def take(bufs, matrix, write):
        out = bufs[8]
        for k in range(GROUP):
            for h in range(2):
                got = out[k, matrix * 64 + h * 32:matrix * 64 + (h + 1) * 32, :].astype(F32)
                write(slice(k * 32, (k + 1) * 32), slice(h * H, (h + 1) * H), got)

    def take_vector(bufs, index, ref, layer):
        s = bufs[6]
        rows = s.shape[0] - 8
        for h in range(2):
            ref[layer:layer + 1, h * H:(h + 1) * H] = (
                s[rows + 2 * index + h:rows + 2 * index + h + 1, :])

    bufs1 = (g1s, g1r, g1a, g1b, g1c, g1d, g1e, g1f, g1g)
    bufs2 = (g2s, g2r, g2a, g2b, g2c, g2d, g2e, g2f, g2g)
    TOT, RED1, RED2 = 16, 18, 23

    def message_half(layer, states):
        value = dot(states, wm[layer]) + bm[layer:layer + 1, :]
        pre[layer] = value
        return (value * sigmoid(value)).astype(BF)

    m1[...] = pair_permutation(B)
    to_t_order(cnt, ct, R)
    states = feat[...]
    st[0] = states
    for layer in range(2):
        messages = message_half(layer, st[layer])
        fill_a(layer, ct, messages[:, :H])
        if layer == 0:
            pl.semaphore_wait(barrier, NP - 1 + B - 1 + NX - 1)
        first_a(layer)
        fill_b(layer, cnt, messages[:, H:])
        first_b(layer)
        if layer == 0:
            totals = jnp.sum(cnt[...].astype(F32), axis=1, keepdims=True).astype(BF)
            line = lax.rem(iota((S, H), 0), PR)
            spreaded = jnp.where(line == iota((S, H), 1), totals.astype(F32), 0.0).astype(BF)
            pick = jnp.where(iota((NP, S), 1) // PR == iota((NP, S), 0), 1.0, 0.0).astype(BF)
            xs[...] = dot(pick, spreaded).reshape(NP, 1, H)
            scatter(xs, xr, TOT, p, plane_peer, NP)
            m2[...] = pair_permutation(NP)
            sel_n[...] = jnp.where(iota((R, S), 0) == t_n[...], 1.0, 0.0).astype(BF)
        base[...] = dot(st[layer], ws[layer]) + bu[layer:layer + 1, :]
        second_b(layer)
        second_a(layer)
        if layer == 0:
            arrived(xr, TOT)
            grid = xr[...].reshape(NP, H).astype(BF)
            lane = iota((B, H), 1)
            turned = jnp.zeros((B, H), F32)
            for k in range(2):
                chosen = jnp.where(lane == 2 * iota((B, H), 0) + k, 1.0, 0.0).astype(BF)
                put = jnp.where(iota((NP, H), 1) == 2 * iota((NP, H), 0) + k, 1.0, 0.0).astype(BF)
                turned = turned + dot(dot_nt(chosen, grid).astype(BF), put)
            ys[...] = turned.reshape(B, 1, H)
            scatter(ys, yr, TOT + 1, b, column_peer, B)
            sel_t[...] = jnp.where(iota((R, S), 0) == t_t[...], 1.0, 0.0).astype(BF)
            selt_n[...] = sel_n[...].T
            selt_t[...] = sel_t[...].T
            arrived(yr, TOT + 1)

            def add(k, total):
                hit = iota((R, H), 0) == t_y[k]
                return total + jnp.where(hit, yr[k], 0.0)
            weight = lax.fori_loop(0, B, add, jnp.zeros((R, H), F32))
            div[...] = jnp.maximum(jnp.sum(weight, axis=1, keepdims=True), 1.0)
        else:
            cnt_n[...] = cnt[...].T
            cnt_t[...] = ct[...].T
        divisor = div[...]
        nm[layer, :, H:] = (dot(sel_t[...], final_b(layer)) / divisor).astype(BF)
        nm[layer, :, :H] = (dot(sel_n[...], final_a(layer)) / divisor).astype(BF)
        value = base[...] + dot(nm[layer], wn[layer])
        upre[layer] = value
        activated = value * sigmoid(value)
        scaling = lax.rsqrt(jnp.mean(activated * activated, axis=-1, keepdims=True) + EPS)
        states = (activated * scaling).astype(BF)
        if layer == 0:
            st[1] = states
        else:
            emb[...] = states

    for turn, layer in ((2, 1), (3, 0)):
        upward = ups[...].astype(F32) if layer == 1 else low[...]
        value = upre[layer]
        activated = value * sigmoid(value)
        scaling = lax.rsqrt(jnp.mean(activated * activated, axis=-1, keepdims=True) + EPS)
        inner = jnp.mean(upward * activated, axis=-1, keepdims=True)
        slope = scaling * upward - activated * (scaling * scaling * scaling) * inner
        slope = slope * silu_slope(value)
        slope_b = slope.astype(BF)
        spread = (dot_nt(slope_b, wn[layer]) / div[...]).astype(BF)
        fill_a(turn, selt_t, spread[:, :H])
        first_a(turn)
        fill_b(turn, selt_n, spread[:, H:])
        first_b(turn)
        update_grad = jnp.sum(slope, axis=0, keepdims=True)
        place(g1s, 0 if layer == 1 else 3, dot_tn(st[layer], slope_b))
        place(g1s, 1 if layer == 1 else 4, dot_tn(nm[layer], slope_b))
        low[...] = dot_nt(slope_b, ws[layer])
        if layer == 1:
            first_update = update_grad
        else:
            place_vectors(g1s, 320, (first_update, first_offset, update_grad))
            reduce_1(bufs1, RED1)
        second_b(turn)
        second_a(turn)
        if layer == 0:
            reduce_2(bufs1, RED1)
            reduce_3(bufs1, RED1)
            reduce_4(bufs1, RED1)
            reduce_5(bufs1, RED1)
        slope_left = dot(cnt_n[...], final_a(turn))
        slope_right = dot(cnt_t[...], final_b(turn))
        pre_slope = jnp.concatenate([slope_left, slope_right], axis=1) * silu_slope(pre[layer])
        pre_b = pre_slope.astype(BF)
        offset_grad = jnp.sum(pre_slope, axis=0, keepdims=True)
        if layer == 1:
            place(g1s, 2, dot_tn(st[1], pre_b))
            first_offset = offset_grad
            low[...] = low[...] + dot_nt(pre_b, wm[1])
        else:
            place(g2s, 0, dot_tn(st[0], pre_b))
            place_vectors(g2s, 64, (offset_grad,))
            reduce_1(bufs2, RED2)
            ing[...] = low[...] + dot_nt(pre_b, wm[0])
    reduce_2(bufs2, RED2)
    reduce_3(bufs2, RED2)

    await_bytes(g1g.at[pl.ds(0, GROUP - 1)], rsem.at[RED1 + 4])
    for matrix, ref, layer in ((0, gs, 1), (1, gn, 1), (2, gm, 1), (3, gs, 0), (4, gn, 0)):
        def write(rows, columns, got, ref=ref, layer=layer):
            ref[layer, rows, columns] = got
        take(bufs1, matrix, write)
    take_vector(bufs1, 0, gu, 1)
    take_vector(bufs1, 1, go, 1)
    take_vector(bufs1, 2, gu, 0)

    reduce_4(bufs2, RED2)
    reduce_5(bufs2, RED2)
    await_bytes(g2g.at[pl.ds(0, GROUP - 1)], rsem.at[RED2 + 4])

    def write_last(rows, columns, got):
        gm[0, rows, columns] = got
    take(bufs2, 0, write_last)
    take_vector(bufs2, 0, go, 0)

    for i in range(4):
        await_bytes(sa.at[i, pl.ds(0, B - 1)], ssem.at[4 * i])
        await_bytes(sb.at[i, pl.ds(0, NP - 1)], ssem.at[4 * i + 1])
        await_bytes(mb.at[i, pl.ds(0, B - 1)], ssem.at[4 * i + 2])
        await_bytes(ma.at[i, pl.ds(0, NP - 1)], ssem.at[4 * i + 3])
    await_bytes(xs.at[pl.ds(0, NP - 1)], ssem.at[TOT])
    await_bytes(ys.at[pl.ds(0, B - 1)], ssem.at[TOT + 1])
    for bufs, slot in ((bufs1, RED1), (bufs2, RED2)):
        await_bytes(bufs[1].at[pl.ds(0, GROUP - 1)], ssem.at[slot])
        await_bytes(bufs[3].at[pl.ds(0, NY - 1)], ssem.at[slot + 1])
        await_bytes(bufs[5].at[pl.ds(0, NZ - 1)], ssem.at[slot + 2])
        await_bytes(bufs[7].at[pl.ds(0, NY - 1)], ssem.at[slot + 3])
        await_bytes(bufs[8].at[pl.ds(0, GROUP - 1)], ssem.at[slot + 4])


def body(NW, NZ, features, upstream, visit_counts, target_rows, wm, bm, ws, wn, bu):
    R = features.shape[0]
    S = visit_counts.shape[0]
    NP, B, NY = NW // NC, NC * NZ, NW // GROUP
    turned = target_rows[0].reshape(NP, B, 2).transpose(1, 0, 2)
    t_t = turned.reshape(1, S)
    t_y = jnp.pad(turned.reshape(B, 1, 2 * NP), ((0, 0), (0, 0), (0, H - 2 * NP)), constant_values=R)

    def sum_buffers(matrices):
        rows = 64 * matrices
        piece = rows // NY
        return [
            pltpu.VMEM((GROUP, rows + 16, H), BF),
            pltpu.VMEM((GROUP, rows + 16, H), BF),
            pltpu.VMEM((NY, piece + 8, H), F32),
            pltpu.VMEM((NY, piece + 8, H), F32),
            pltpu.VMEM((piece + 8, H), F32),
            pltpu.VMEM((NZ, piece + 8, H), F32),
            pltpu.VMEM((piece + 8, H), F32),
            pltpu.VMEM((NY, piece, H), F32),
            pltpu.VMEM((GROUP, rows, H), BF),
        ]

    column = pltpu.VMEM((4, B, 2 * NP, H), BF)
    plane = pltpu.VMEM((4, NP, 2 * B, H), BF)
    scratch = [
        pltpu.VMEM((S, R), BF), pltpu.VMEM((R, S), BF), pltpu.VMEM((R, S), BF),
        pltpu.VMEM((R, S), BF), pltpu.VMEM((R, S), BF),
        pltpu.VMEM((S, R), BF), pltpu.VMEM((S, R), BF),
        pltpu.VMEM((16 * B, 16 * B), BF), pltpu.VMEM((16 * NP, 16 * NP), BF),
        pltpu.VMEM((2, R, F), F32), pltpu.VMEM((2, R, F), F32),
        pltpu.VMEM((2, R, F), BF), pltpu.VMEM((2, R, F), BF),
        pltpu.VMEM((R, F), F32), pltpu.VMEM((R, F), F32), pltpu.VMEM((R, 1), F32),
        column, column, plane, plane, plane, plane, column, column,
        pltpu.VMEM((NP, 1, H), F32), pltpu.VMEM((NP, 1, H), F32),
        pltpu.VMEM((B, 1, H), F32), pltpu.VMEM((B, 1, H), F32),
    ] + sum_buffers(5) + sum_buffers(1) + [
        pltpu.SemaphoreType.DMA((28,)), pltpu.SemaphoreType.DMA((28,)),
    ]
    vmem = pl.BlockSpec(memory_space=pltpu.VMEM)
    square = jax.ShapeDtypeStruct((2, F, F), F32)
    line = jax.ShapeDtypeStruct((2, F), F32)
    return pl.pallas_call(
        functools.partial(kernel, NW, NZ, R),
        out_shape=(
            jax.ShapeDtypeStruct((R, F), BF), jax.ShapeDtypeStruct((R, F), F32),
            square, line, square, square, line,
        ),
        in_specs=[vmem] * 11,
        out_specs=[vmem] * 7,
        scratch_shapes=scratch,
        compiler_params=pltpu.CompilerParams(
            collective_id=0, has_side_effects=True, vmem_limit_bytes=58 * 2**20),
        cost_estimate=pl.CostEstimate(flops=12 * 2**30, bytes_accessed=2**23, transcendentals=2**20),
    )(features, upstream, visit_counts, target_rows, t_t, t_y, wm, bm, ws, wn, bu)


def solution(mesh):
    split = P(("wide", "narrow"), None)
    in_specs = (split, split, split, split, P(), P(), P(), P(), P())
    out_specs = (split, split, P(), P(), P(), P(), P())
    run = functools.partial(body, mesh.shape["wide"], mesh.shape["narrow"])
    return jax.shard_map(run, mesh=mesh, in_specs=in_specs, out_specs=out_specs, check_vma=False)
```

```python
import functools

import jax
import jax.numpy as jnp
from jax import lax
from jax.experimental import pallas as pl
from jax.experimental.pallas import tpu as pltpu
from jax.sharding import PartitionSpec as P

F = 256
H = 128
NX = 4
NC = 2
GROUP = NX * NC
EPS = 1e-05
MATRICES = (2, 3, 1)
BF = jnp.bfloat16
F32 = jnp.float32
MESH = pl.DeviceIdType.MESH


def sigmoid(v):
    return 1.0 / (1.0 + jnp.exp(-v))


def silu_slope(v):
    sigma = sigmoid(v)
    return sigma * (1.0 + v * (1.0 - sigma))


def dot(a, b):
    return jnp.dot(a, b, preferred_element_type=F32)


def dot_nt(a, b):
    return lax.dot_general(a, b, (((1,), (1,)), ((), ())), preferred_element_type=F32)


def dot_tn(a, b):
    return lax.dot_general(a, b, (((0,), (0,)), ((), ())), preferred_element_type=F32)


def iota(shape, dim):
    return lax.broadcasted_iota(jnp.int32, shape, dim)


def pair_permutation(blocks):
    n = 16 * blocks
    out = iota((n, n), 0)
    source = ((out // 2) % 8) * (2 * blocks) + (out // 16) * 2 + out % 2
    return jnp.where(iota((n, n), 1) == source, 1.0, 0.0).astype(BF)


def alternate(t, n):
    s = (t + 1) // 2
    return lax.rem(s + (1 - lax.rem(t, 2)) * (n - 2 * s), n)


def kernel(
    NW, NZ, R,
    feat_in, ups_in, cnt_in, t_n, wm_in, bm, ws_in, wn_in, bu,
    emb, ing, gm, go, gs, gn, gu,
    feat, ups, cnt, wm, ws, wn,
    ct, cnt_n, cnt_t, sel_n, sel_t, selt_n, selt_t, m1, m2,
    pre, upre, st, nm, base, low, div,
    sa, za, ma, xa, sb, xb, mb, zb,
    xs, xr, ys, yr,
    *rest,
):
    NP = NW // NC
    NY = NP // NX
    B = NC * NZ
    PR, BR = 2 * B, 2 * NP
    S = NP * PR
    wide = lax.axis_index("wide")
    z = lax.axis_index("narrow")
    p, c = wide // NC, lax.rem(wide, NC)
    y, x = p // NX, lax.rem(p, NX)
    q = lax.rem(wide, GROUP)
    b = c * NZ + z

    def plane_peer(d):
        dy = alternate(d // NX, NY)
        yy, xx = lax.rem(y + dy, NY), lax.rem(x + lax.rem(d, NX), NX)
        pp = yy * NX + xx
        return pp, (pp * NC + c, z)

    def column_peer(j):
        dz = alternate(j // 2, NZ)
        cc, zz = lax.rem(c + lax.rem(j, 2), NC), lax.rem(z + dz, NZ)
        return cc * NZ + zz, (p * NC + cc, zz)

    def group_peer(j):
        qq = lax.rem(q + j, GROUP)
        return qq, (y * GROUP + qq, z)

    def row_peer(j):
        yy = lax.rem(y + j, NY)
        return yy, (yy * GROUP + q, z)

    def ring_peer(j):
        zz = lax.rem(z + j, NZ)
        return zz, (wide, zz)

    def send(src, dst, slot, target):
        pltpu.make_async_remote_copy(
            src_ref=src, dst_ref=dst, send_sem=ssem.at[slot], recv_sem=rsem.at[slot],
            device_id=target, device_id_type=MESH,
        ).start()

    def scatter(src, dst, slot, mine, peer, n):
        def step(i, _):
            theirs, target = peer(n - i)
            send(src.at[theirs], dst.at[mine], slot, target)
            return _
        lax.fori_loop(1, n, step, 0)
        dst[pl.ds(mine, 1)] = src[pl.ds(mine, 1)]

    def spread_out(src, dst, slot, mine, peer, n):
        def step(i, _):
            send(src, dst.at[mine], slot, peer(n - i)[1])
            return _
        lax.fori_loop(1, n, step, 0)
        dst[pl.ds(mine, 1)] = src[...][None]

    def await_bytes(ref, sem):
        pltpu.make_async_copy(ref, ref, sem).wait()

    def arrived(dst, slot):
        await_bytes(dst.at[pl.ds(0, dst.shape[0] - 1)], rsem.at[slot])

    groups, (lsem, ssem, rsem) = (rest[:9], rest[9:18], rest[18:27]), rest[27:]
    loads = [
        pltpu.make_async_copy(src, dst, lsem.at[k])
        for k, (src, dst) in enumerate((
            (cnt_in, cnt), (feat_in, feat), (wm_in, wm), (ws_in, ws), (wn_in, wn), (ups_in, ups)))
    ]
    for load in loads:
        load.start()

    barrier = pltpu.get_barrier_semaphore()

    def greet(peer, first, last):
        def step(i, _):
            pl.semaphore_signal(barrier, inc=1, device_id=peer(i)[1], device_id_type=MESH)
            return _
        lax.fori_loop(first, last, step, 0)

    greet(plane_peer, 1, NP)
    greet(column_peer, 1, B)
    greet(lambda i: (i, ((y * NX + lax.rem(x + i, NX)) * NC + (1 - c), z)), 1, NX)

    def to_t_order(src, dst, width):
        for o in range(NP // 8):
            got = dot(m1[...], src[o * 8 * PR:(o + 1) * 8 * PR, :]).astype(BF)
            got = got.reshape(B, 16, width)
            for i in range(B):
                dst[i * BR + o * 16:i * BR + (o + 1) * 16, :] = got[i]

    def shuffle_b(i):
        for o in range(NP // 8):
            got = dot(m1[...], xb[i, o * 8:(o + 1) * 8].reshape(8 * PR, H)).astype(BF)
            mb[i, :, o * 16:(o + 1) * 16, :] = got.reshape(B, 16, H)

    def shuffle_a(i):
        for o in range(B // 8):
            got = dot(m2[...], za[i, o * 8:(o + 1) * 8].reshape(8 * BR, H)).astype(BF)
            ma[i, :, o * 16:(o + 1) * 16, :] = got.reshape(NP, 16, H)

    def fill_a(i, left, right):
        n = max(1, B // 6)
        rows = S // n
        for k in range(n):
            got = dot(left[k * rows:(k + 1) * rows, :], right).astype(BF)
            sa[i, k * (B // n):(k + 1) * (B // n)] = got.reshape(B // n, BR, H)

    def fill_b(i, left, right):
        n = NP // 8
        rows = S // n
        for k in range(n):
            got = dot(left[k * rows:(k + 1) * rows, :], right).astype(BF)
            sb[i, k * 8:(k + 1) * 8] = got.reshape(8, PR, H)

    def first_a(i):
        scatter(sa.at[i], za.at[i], 4 * i, b, column_peer, B)

    def first_b(i):
        scatter(sb.at[i], xb.at[i], 4 * i + 1, p, plane_peer, NP)

    def second_b(i):
        arrived(xb.at[i], 4 * i + 1)
        shuffle_b(i)
        scatter(mb.at[i], zb.at[i], 4 * i + 2, b, column_peer, B)

    def second_a(i):
        arrived(za.at[i], 4 * i)
        shuffle_a(i)
        scatter(ma.at[i], xa.at[i], 4 * i + 3, p, plane_peer, NP)

    def final_a(i):
        arrived(xa.at[i], 4 * i + 3)
        return xa[i].reshape(S, H)

    def final_b(i):
        arrived(zb.at[i], 4 * i + 2)
        return zb[i].reshape(S, H)

    def place(buf, matrix, value):
        g = value.astype(BF)
        for k in range(GROUP):
            for h in range(2):
                buf[k, matrix * 64 + h * 32:matrix * 64 + (h + 1) * 32, :] = (
                    g[k * 32:(k + 1) * 32, h * H:(h + 1) * H])

    def place_vectors(buf, rows, vectors):
        tile = jnp.zeros((16, H), F32)
        line = iota((16, H), 0)
        for v, vec in enumerate(vectors):
            for h in range(2):
                tile = jnp.where(line == 2 * v + h, vec[:, h * H:(h + 1) * H], tile)
        for k in range(GROUP):
            buf[k, rows:rows + 16, :] = tile.astype(BF)

    def reduce_1(g):
        scatter(groups[g][0], groups[g][1], RED + 5 * g, q, group_peer, GROUP)

    def extra(g):
        return groups[g][0].shape[1] - 64 * MATRICES[g]

    def reduce_2(g):
        r, a = groups[g][1], groups[g][2]
        arrived(r, RED + 5 * g)
        rows, piece = 64 * MATRICES[g], 64 * MATRICES[g] // NY
        total = r[0].astype(F32)
        for k in range(1, GROUP):
            total = total + r[k].astype(F32)
        for k in range(NY):
            part = total[k * piece:(k + 1) * piece]
            if extra(g):
                part = jnp.concatenate([part, total[rows:rows + 8]], axis=0)
            a[k] = part.astype(BF)
        scatter(a, groups[g][3], RED + 5 * g + 1, y, row_peer, NY)

    def reduce_3(g):
        r, s = groups[g][3], groups[g][4]
        arrived(r, RED + 5 * g + 1)
        total = r[0].astype(F32)
        for k in range(1, NY):
            total = total + r[k].astype(F32)
        s[...] = total.astype(BF)
        spread_out(s, groups[g][5], RED + 5 * g + 2, z, ring_peer, NZ)

    def reduce_4(g):
        r, s = groups[g][5], groups[g][6]
        arrived(r, RED + 5 * g + 2)
        total = r[0].astype(F32)
        for k in range(1, NZ):
            total = total + r[k].astype(F32)
        s[...] = total.astype(BF)
        spread_out(s, groups[g][7], RED + 5 * g + 3, y, row_peer, NY)

    def reduce_5(g):
        r, out = groups[g][7], groups[g][8]
        arrived(r, RED + 5 * g + 3)
        piece = 64 * MATRICES[g] // NY
        chunk = jnp.concatenate([r[k].astype(F32)[:piece] for k in range(NY)], axis=0)
        out[pl.ds(q, 1)] = chunk.astype(BF)[None]

        def step(i, _):
            send(out.at[q], out.at[q], RED + 5 * g + 4, group_peer(GROUP - i)[1])
            return _
        lax.fori_loop(1, GROUP, step, 0)

    def result(g, targets):
        out = groups[g][8]
        arrived(out, RED + 5 * g + 4)
        for m, (ref, layer) in enumerate(targets):
            for k in range(GROUP):
                for h in range(2):
                    got = out[k, m * 64 + h * 32:m * 64 + (h + 1) * 32, :].astype(F32)
                    ref[layer, k * 32:(k + 1) * 32, h * H:(h + 1) * H] = got

    def vectors(g, targets):
        s = groups[g][6]
        tile = s[s.shape[0] - 16:, :].astype(F32)[8:]
        for v, (ref, layer) in enumerate(targets):
            for h in range(2):
                ref[layer:layer + 1, h * H:(h + 1) * H] = tile[2 * v + h:2 * v + h + 1, :]

    TOT, RED = 16, 18

    def message_half(layer, states):
        value = dot(states, wm[layer]) + bm[layer:layer + 1, :]
        pre[layer] = value
        return (value * sigmoid(value)).astype(BF)

    m1[...] = pair_permutation(B)
    loads[0].wait()
    to_t_order(cnt, ct, R)
    loads[1].wait()
    loads[2].wait()
    st[0] = feat[...]
    for layer in range(2):
        messages = message_half(layer, st[layer])
        fill_a(layer, ct, messages[:, :H])
        if layer == 0:
            pl.semaphore_wait(barrier, NP - 1 + B - 1 + NX - 1)
        first_a(layer)
        fill_b(layer, cnt, messages[:, H:])
        first_b(layer)
        if layer == 0:
            totals = jnp.sum(cnt[...].astype(F32), axis=1, keepdims=True).astype(BF)
            line = lax.rem(iota((S, H), 0), PR)
            spreaded = jnp.where(line == iota((S, H), 1), totals.astype(F32), 0.0).astype(BF)
            pick = jnp.where(iota((NP, S), 1) // PR == iota((NP, S), 0), 1.0, 0.0).astype(BF)
            xs[...] = dot(pick, spreaded).reshape(NP, 1, H)
            scatter(xs, xr, TOT, p, plane_peer, NP)
            m2[...] = pair_permutation(NP)
            sel_n[...] = jnp.where(iota((R, S), 0) == t_n[...], 1.0, 0.0).astype(BF)
            loads[3].wait()
            loads[4].wait()
            loads[5].wait()
        base[...] = dot(st[layer], ws[layer]) + bu[layer:layer + 1, :]
        second_b(layer)
        second_a(layer)
        if layer == 0:
            arrived(xr, TOT)
            grid = xr[...].reshape(NP, H).astype(BF)
            lane = iota((B, H), 1)
            turned = jnp.zeros((B, H), F32)
            for k in range(2):
                chosen = jnp.where(lane == 2 * iota((B, H), 0) + k, 1.0, 0.0).astype(BF)
                put = iota((NP, H), 1) % BR == 2 * iota((NP, H), 0) + k
                put = jnp.where(put, 1.0, 0.0).astype(BF)
                turned = turned + dot(dot_nt(chosen, grid).astype(BF), put)
            ys[...] = turned.reshape(B, 1, H)
            scatter(ys, yr, TOT + 1, b, column_peer, B)
            selt_n[...] = sel_n[...].T
            to_t_order(selt_n, selt_t, R)
            sel_t[...] = selt_t[...].T
            arrived(yr, TOT + 1)
            per = H // BR
            place_of = iota((1, H), 1) // BR
            parts = []
            for k in range(0, B, per):
                part = yr[k]
                for j in range(1, per):
                    part = jnp.where(place_of == j, yr[k + j], part)
                parts.append(part)
            row = jnp.broadcast_to(jnp.concatenate(parts, axis=1), (16, S)).astype(BF)
            weight = dot_nt(sel_t[...], row)
            div[...] = jnp.maximum(weight[:, 0:1], 1.0)
        else:
            cnt_n[...] = cnt[...].T
            cnt_t[...] = ct[...].T
        divisor = div[...]
        nm[layer, :, :H] = (dot(sel_n[...], final_a(layer)) / divisor).astype(BF)
        nm[layer, :, H:] = (dot(sel_t[...], final_b(layer)) / divisor).astype(BF)
        value = base[...] + dot(nm[layer], wn[layer])
        upre[layer] = value
        activated = value * sigmoid(value)
        scaling = lax.rsqrt(jnp.mean(activated * activated, axis=-1, keepdims=True) + EPS)
        states = (activated * scaling).astype(BF)
        if layer == 0:
            st[1] = states
        else:
            emb[...] = states

    for turn, layer in ((2, 1), (3, 0)):
        upward = ups[...].astype(F32) if layer == 1 else low[...]
        value = upre[layer]
        activated = value * sigmoid(value)
        scaling = lax.rsqrt(jnp.mean(activated * activated, axis=-1, keepdims=True) + EPS)
        inner = jnp.mean(upward * activated, axis=-1, keepdims=True)
        slope = scaling * upward - activated * (scaling * scaling * scaling) * inner
        slope = slope * silu_slope(value)
        slope_b = slope.astype(BF)
        spread = (dot_nt(slope_b, wn[layer]) / div[...]).astype(BF)
        fill_a(turn, selt_t, spread[:, :H])
        first_a(turn)
        fill_b(turn, selt_n, spread[:, H:])
        first_b(turn)
        update_grad = jnp.sum(slope, axis=0, keepdims=True)
        if layer == 1:
            first_update = update_grad
            place(groups[0][0], 0, dot_tn(st[1], slope_b))
            place(groups[0][0], 1, dot_tn(nm[1], slope_b))
            reduce_1(0)
        else:
            first_offset = jnp.sum(base[...], axis=0, keepdims=True)
            place(groups[1][0], 0, dot_tn(st[1], first_pre_b))
            place(groups[1][0], 1, dot_tn(st[0], slope_b))
            place(groups[1][0], 2, dot_tn(nm[0], slope_b))
            place_vectors(groups[1][0], 192, (first_update, first_offset, update_grad))
            reduce_1(1)
            reduce_4(0)
        low[...] = dot_nt(slope_b, ws[layer])
        second_b(turn)
        reduce_2(0 if layer == 1 else 1)
        second_a(turn)
        if layer == 1:
            reduce_3(0)
        else:
            reduce_3(1)
            reduce_5(0)
        slope_left = dot(cnt_n[...], final_a(turn))
        slope_right = dot(cnt_t[...], final_b(turn))
        pre_slope = jnp.concatenate([slope_left, slope_right], axis=1) * silu_slope(pre[layer])
        pre_b = pre_slope.astype(BF)
        if layer == 1:
            low[...] = low[...] + dot_nt(pre_b, wm[1])
            base[...] = pre_slope
            first_pre_b = pre_b
        else:
            place(groups[2][0], 0, dot_tn(st[0], pre_b))
            place_vectors(groups[2][0], 64, (jnp.sum(pre_slope, axis=0, keepdims=True),))
            reduce_1(2)
            reduce_4(1)
            ing[...] = low[...] + dot_nt(pre_b, wm[0])
    reduce_2(2)
    reduce_5(1)
    vectors(1, ((gu, 1), (go, 1), (gu, 0)))
    reduce_3(2)
    result(0, ((gs, 1), (gn, 1)))
    reduce_4(2)
    result(1, ((gm, 1), (gs, 0), (gn, 0)))
    vectors(2, ((go, 0),))
    reduce_5(2)
    result(2, ((gm, 0),))

    for i in range(4):
        await_bytes(sa.at[i, pl.ds(0, B - 1)], ssem.at[4 * i])
        await_bytes(sb.at[i, pl.ds(0, NP - 1)], ssem.at[4 * i + 1])
        await_bytes(mb.at[i, pl.ds(0, B - 1)], ssem.at[4 * i + 2])
        await_bytes(ma.at[i, pl.ds(0, NP - 1)], ssem.at[4 * i + 3])
    await_bytes(xs.at[pl.ds(0, NP - 1)], ssem.at[TOT])
    await_bytes(ys.at[pl.ds(0, B - 1)], ssem.at[TOT + 1])
    for g, bufs in enumerate(groups):
        for stage, (k, n) in enumerate(((1, GROUP), (3, NY), (5, NZ), (7, NY), (8, GROUP))):
            await_bytes(bufs[k].at[pl.ds(0, n - 1)], ssem.at[RED + 5 * g + stage])


def hand_on(*refs):
    n = len(refs) // 2
    copies = [
        pltpu.make_async_copy(refs[k], refs[n + k], refs[-1].at[k]) for k in range(n)]
    for copy in copies:
        copy.start()
    for copy in copies:
        copy.wait()


def body(NW, NZ, features, upstream, visit_counts, target_rows, wm, bm, ws, wn, bu):
    R = features.shape[0]
    S = visit_counts.shape[0]
    NP, B, NY = NW // NC, NC * NZ, NW // GROUP

    def sum_buffers(matrices, extra):
        rows = 64 * matrices
        piece = rows // NY + extra // 2
        return [
            pltpu.VMEM((GROUP, rows + extra, H), BF),
            pltpu.VMEM((GROUP, rows + extra, H), BF),
            pltpu.VMEM((NY, piece, H), BF),
            pltpu.VMEM((NY, piece, H), BF),
            pltpu.VMEM((piece, H), BF),
            pltpu.VMEM((NZ, piece, H), BF),
            pltpu.VMEM((piece, H), BF),
            pltpu.VMEM((NY, piece, H), BF),
            pltpu.VMEM((GROUP, rows, H), BF),
        ]

    column = pltpu.VMEM((4, B, 2 * NP, H), BF)
    plane = pltpu.VMEM((4, NP, 2 * B, H), BF)
    scratch = [
        pltpu.VMEM((R, F), BF), pltpu.VMEM((R, F), BF), pltpu.VMEM((S, R), BF),
        pltpu.VMEM((2, F, F), BF), pltpu.VMEM((2, F, F), BF), pltpu.VMEM((2, F, F), BF),
        pltpu.VMEM((S, R), BF), pltpu.VMEM((R, S), BF), pltpu.VMEM((R, S), BF),
        pltpu.VMEM((R, S), BF), pltpu.VMEM((R, S), BF),
        pltpu.VMEM((S, R), BF), pltpu.VMEM((S, R), BF),
        pltpu.VMEM((16 * B, 16 * B), BF), pltpu.VMEM((16 * NP, 16 * NP), BF),
        pltpu.VMEM((2, R, F), F32), pltpu.VMEM((2, R, F), F32),
        pltpu.VMEM((2, R, F), BF), pltpu.VMEM((2, R, F), BF),
        pltpu.VMEM((R, F), F32), pltpu.VMEM((R, F), F32), pltpu.VMEM((R, 1), F32),
        column, column, plane, plane, plane, plane, column, column,
        pltpu.VMEM((NP, 1, H), F32), pltpu.VMEM((NP, 1, H), F32),
        pltpu.VMEM((B, 1, H), F32), pltpu.VMEM((B, 1, H), F32),
    ] + sum_buffers(MATRICES[0], 0) + sum_buffers(MATRICES[1], 16) + sum_buffers(MATRICES[2], 16) + [
        pltpu.SemaphoreType.DMA((6,)), pltpu.SemaphoreType.DMA((33,)), pltpu.SemaphoreType.DMA((33,)),
    ]
    vmem = pl.BlockSpec(memory_space=pltpu.VMEM)
    square = jax.ShapeDtypeStruct((2, F, F), F32)
    line = jax.ShapeDtypeStruct((2, F), F32)
    shapes = (
        jax.ShapeDtypeStruct((R, F), BF), jax.ShapeDtypeStruct((R, F), F32),
        square, line, square, square, line,
    )
    anywhere = pl.BlockSpec(memory_space=pl.ANY)
    outs = pl.pallas_call(
        functools.partial(kernel, NW, NZ, R),
        out_shape=shapes,
        in_specs=[anywhere, anywhere, anywhere, vmem, anywhere, vmem, anywhere, anywhere, vmem],
        out_specs=[vmem] * 7,
        scratch_shapes=scratch,
        compiler_params=pltpu.CompilerParams(
            collective_id=0, has_side_effects=True, vmem_limit_bytes=58 * 2**20),
        cost_estimate=pl.CostEstimate(flops=12 * 2**30, bytes_accessed=2**23, transcendentals=2**20),
    )(features, upstream, visit_counts, target_rows, wm, bm, ws, wn, bu)
    return pl.pallas_call(
        hand_on,
        out_shape=shapes,
        in_specs=[anywhere] * len(shapes),
        out_specs=[anywhere] * len(shapes),
        scratch_shapes=[pltpu.SemaphoreType.DMA((len(shapes),))],
        cost_estimate=pl.CostEstimate(flops=0, bytes_accessed=2**22, transcendentals=0),
    )(*outs)


def solution(mesh):
    split = P(("wide", "narrow"), None)
    in_specs = (split, split, split, split, P(), P(), P(), P(), P())
    out_specs = (split, split, P(), P(), P(), P(), P())
    run = functools.partial(body, mesh.shape["wide"], mesh.shape["narrow"])
    return jax.shard_map(run, mesh=mesh, in_specs=in_specs, out_specs=out_specs, check_vma=False)
```

```python
import functools

import jax
import jax.numpy as jnp
from jax import lax
from jax.experimental import pallas as pl
from jax.experimental.pallas import tpu as pltpu
from jax.sharding import PartitionSpec as P

F = 256
H = 128
NX = 4
NC = 2
GROUP = NX * NC
EPS = 1e-05
MATRICES = (2, 3, 1)
BF = jnp.bfloat16
F32 = jnp.float32
MESH = pl.DeviceIdType.MESH


def sigmoid(v):
    return 1.0 / (1.0 + jnp.exp(-v))


def dot(a, b):
    return jnp.dot(a, b, preferred_element_type=F32)


def dot_nt(a, b):
    return lax.dot_general(a, b, (((1,), (1,)), ((), ())), preferred_element_type=F32)


def dot_tn(a, b):
    return lax.dot_general(a, b, (((0,), (0,)), ((), ())), preferred_element_type=F32)


def iota(shape, dim):
    return lax.broadcasted_iota(jnp.int32, shape, dim)


def pair_permutation(blocks):
    n = 16 * blocks
    out = iota((n, n), 0)
    source = ((out // 2) % 8) * (2 * blocks) + (out // 16) * 2 + out % 2
    return jnp.where(iota((n, n), 1) == source, 1.0, 0.0).astype(BF)


def alternate(t, n):
    s = (t + 1) // 2
    return lax.rem(s + (1 - lax.rem(t, 2)) * (n - 2 * s), n)


def kernel(
    NW, NZ, R,
    feat_in, ups_in, cnt_in, t_n, wm_in, bm, ws_in, wn_in, bu,
    emb, ing, gm, go, gs, gn, gu,
    feat, ups, cnt, wm, ws, wn,
    ct, cnt_n, cnt_t, sel_n, sel_t, selt_n, selt_t, m1, m2,
    dpre, act, dsl, scl, st, st_t, nm, pb, base, low, inv,
    sa, za, ma, xa, sb, xb, mb, zb,
    xs, xr, ys, yr,
    *rest,
):
    NP = NW // NC
    NY = NP // NX
    B = NC * NZ
    PR, BR = 2 * B, 2 * NP
    S = NP * PR
    wide = lax.axis_index("wide")
    z = lax.axis_index("narrow")
    p, c = wide // NC, lax.rem(wide, NC)
    y, x = p // NX, lax.rem(p, NX)
    q = lax.rem(wide, GROUP)
    b = c * NZ + z

    def plane_peer(d):
        dy = alternate(d // NX, NY)
        yy, xx = lax.rem(y + dy, NY), lax.rem(x + lax.rem(d, NX), NX)
        pp = yy * NX + xx
        return pp, (pp * NC + c, z)

    def column_peer(j):
        dz = alternate(j // 2, NZ)
        cc, zz = lax.rem(c + lax.rem(j, 2), NC), lax.rem(z + dz, NZ)
        return cc * NZ + zz, (p * NC + cc, zz)

    def group_peer(j):
        qq = lax.rem(q + j, GROUP)
        return qq, (y * GROUP + qq, z)

    def row_peer(j):
        yy = lax.rem(y + j, NY)
        return yy, (yy * GROUP + q, z)

    def ring_peer(j):
        zz = lax.rem(z + j, NZ)
        return zz, (wide, zz)

    def send(src, dst, slot, target):
        pltpu.make_async_remote_copy(
            src_ref=src, dst_ref=dst, send_sem=ssem.at[slot], recv_sem=rsem.at[slot],
            device_id=target, device_id_type=MESH,
        ).start()

    def scatter(src, dst, slot, mine, peer, n):
        def step(i, _):
            theirs, target = peer(n - i)
            send(src.at[theirs], dst.at[mine], slot, target)
            return _
        lax.fori_loop(1, n, step, 0)
        dst[pl.ds(mine, 1)] = src[pl.ds(mine, 1)]

    def spread_out(src, dst, slot, mine, peer, n):
        def step(i, _):
            send(src, dst.at[mine], slot, peer(n - i)[1])
            return _
        lax.fori_loop(1, n, step, 0)
        dst[pl.ds(mine, 1)] = src[...][None]

    def await_bytes(ref, sem):
        pltpu.make_async_copy(ref, ref, sem).wait()

    def arrived(dst, slot):
        await_bytes(dst.at[pl.ds(0, dst.shape[0] - 1)], rsem.at[slot])

    groups, (lsem, ssem, rsem) = (rest[:9], rest[9:18], rest[18:27]), rest[27:]
    loads = [
        pltpu.make_async_copy(src, dst, lsem.at[k])
        for k, (src, dst) in enumerate((
            (cnt_in, cnt), (feat_in, feat), (wm_in, wm), (ws_in, ws), (wn_in, wn), (ups_in, ups)))
    ]
    for load in loads:
        load.start()

    barrier = pltpu.get_barrier_semaphore()

    def greet(peer, first, last):
        def step(i, _):
            pl.semaphore_signal(barrier, inc=1, device_id=peer(i)[1], device_id_type=MESH)
            return _
        lax.fori_loop(first, last, step, 0)

    greet(plane_peer, 1, NP)
    greet(column_peer, 1, B)
    greet(lambda i: (i, ((y * NX + lax.rem(x + i, NX)) * NC + (1 - c), z)), 1, NX)

    def to_t_order(src, dst, width):
        for o in range(NP // 8):
            got = dot(m1[...], src[o * 8 * PR:(o + 1) * 8 * PR, :]).astype(BF)
            got = got.reshape(B, 16, width)
            for i in range(B):
                dst[i * BR + o * 16:i * BR + (o + 1) * 16, :] = got[i]

    def shuffle_b(i):
        for o in range(NP // 8):
            got = dot(m1[...], xb[i, o * 8:(o + 1) * 8].reshape(8 * PR, H)).astype(BF)
            mb[i, :, o * 16:(o + 1) * 16, :] = got.reshape(B, 16, H)

    def shuffle_a(i):
        for o in range(B // 8):
            got = dot(m2[...], za[i, o * 8:(o + 1) * 8].reshape(8 * BR, H)).astype(BF)
            ma[i, :, o * 16:(o + 1) * 16, :] = got.reshape(NP, 16, H)

    def fill_a(i, left, right):
        n = max(1, B // 6)
        rows = S // n
        for k in range(n):
            got = dot(left[k * rows:(k + 1) * rows, :], right).astype(BF)
            sa[i, k * (B // n):(k + 1) * (B // n)] = got.reshape(B // n, BR, H)

    def fill_b(i, left, right):
        n = NP // 8
        rows = S // n
        for k in range(n):
            got = dot(left[k * rows:(k + 1) * rows, :], right).astype(BF)
            sb[i, k * 8:(k + 1) * 8] = got.reshape(8, PR, H)

    def first_a(i):
        scatter(sa.at[i], za.at[i], 4 * i, b, column_peer, B)

    def first_b(i):
        scatter(sb.at[i], xb.at[i], 4 * i + 1, p, plane_peer, NP)

    def second_b(i):
        arrived(xb.at[i], 4 * i + 1)
        shuffle_b(i)
        scatter(mb.at[i], zb.at[i], 4 * i + 2, b, column_peer, B)

    def second_a(i):
        arrived(za.at[i], 4 * i)
        shuffle_a(i)
        scatter(ma.at[i], xa.at[i], 4 * i + 3, p, plane_peer, NP)

    def final_a(i):
        arrived(xa.at[i], 4 * i + 3)
        return xa[i].reshape(S, H)

    def final_b(i):
        arrived(zb.at[i], 4 * i + 2)
        return zb[i].reshape(S, H)

    def place_half(buf, matrix, h, value):
        g = value.astype(BF)
        for k in range(GROUP):
            buf[k, matrix * 64 + h * 32:matrix * 64 + (h + 1) * 32, :] = g[k * 32:(k + 1) * 32]

    def place(buf, matrix, value):
        for h in range(2):
            place_half(buf, matrix, h, value[:, h * H:(h + 1) * H])

    def place_vectors(buf, rows, vectors):
        tile = jnp.zeros((16, H), F32)
        line = iota((16, H), 0)
        for v, vec in enumerate(vectors):
            for h in range(2):
                tile = jnp.where(line == 2 * v + h, vec[:, h * H:(h + 1) * H], tile)
        for k in range(GROUP):
            buf[k, rows:rows + 16, :] = tile.astype(BF)

    def reduce_1(g):
        scatter(groups[g][0], groups[g][1], RED + 5 * g, q, group_peer, GROUP)

    def extra(g):
        return groups[g][0].shape[1] - 64 * MATRICES[g]

    def reduce_2(g):
        r, a = groups[g][1], groups[g][2]
        arrived(r, RED + 5 * g)
        rows, piece = 64 * MATRICES[g], 64 * MATRICES[g] // NY
        total = r[0].astype(F32)
        for k in range(1, GROUP):
            total = total + r[k].astype(F32)
        for k in range(NY):
            part = total[k * piece:(k + 1) * piece]
            if extra(g):
                part = jnp.concatenate([part, total[rows:rows + 8]], axis=0)
            a[k] = part.astype(BF)
        scatter(a, groups[g][3], RED + 5 * g + 1, y, row_peer, NY)

    def reduce_3(g):
        r, s = groups[g][3], groups[g][4]
        arrived(r, RED + 5 * g + 1)
        total = r[0].astype(F32)
        for k in range(1, NY):
            total = total + r[k].astype(F32)
        s[...] = total.astype(BF)
        spread_out(s, groups[g][5], RED + 5 * g + 2, z, ring_peer, NZ)

    def reduce_4(g):
        r, s = groups[g][5], groups[g][6]
        arrived(r, RED + 5 * g + 2)
        total = r[0].astype(F32)
        for k in range(1, NZ):
            total = total + r[k].astype(F32)
        s[...] = total.astype(BF)
        spread_out(s, groups[g][7], RED + 5 * g + 3, y, row_peer, NY)

    def reduce_5(g):
        r, out = groups[g][7], groups[g][8]
        arrived(r, RED + 5 * g + 3)
        piece = 64 * MATRICES[g] // NY
        chunk = jnp.concatenate([r[k].astype(F32)[:piece] for k in range(NY)], axis=0)
        out[pl.ds(q, 1)] = chunk.astype(BF)[None]

        def step(i, _):
            send(out.at[q], out.at[q], RED + 5 * g + 4, group_peer(GROUP - i)[1])
            return _
        lax.fori_loop(1, GROUP, step, 0)

    def result(g, targets):
        out = groups[g][8]
        arrived(out, RED + 5 * g + 4)
        for m, (ref, layer) in enumerate(targets):
            for k in range(GROUP):
                for h in range(2):
                    got = out[k, m * 64 + h * 32:m * 64 + (h + 1) * 32, :].astype(F32)
                    ref[layer, k * 32:(k + 1) * 32, h * H:(h + 1) * H] = got

    def vectors(g, targets):
        s = groups[g][6]
        tile = s[s.shape[0] - 16:, :].astype(F32)[8:]
        for v, (ref, layer) in enumerate(targets):
            for h in range(2):
                ref[layer:layer + 1, h * H:(h + 1) * H] = tile[2 * v + h:2 * v + h + 1, :]

    TOT, RED = 16, 18

    def message_half(layer, half):
        value = dot(st[layer], wm[layer, :, half]) + bm[layer:layer + 1, half]
        sigma = sigmoid(value)
        dpre[layer, :, half] = sigma * (1.0 + value * (1.0 - sigma))
        return (value * sigma).astype(BF)

    def settle(value):
        sigma = sigmoid(value)
        activated = value * sigma
        scaling = lax.rsqrt(jnp.mean(activated * activated, axis=-1, keepdims=True) + EPS)
        return activated, sigma * (1.0 + value * (1.0 - sigma)), scaling

    LEFT, RIGHT = slice(0, H), slice(H, F)

    m1[...] = pair_permutation(B)
    loads[0].wait()
    to_t_order(cnt, ct, R)
    loads[1].wait()
    loads[2].wait()
    st[0] = feat[...]
    for layer in range(2):
        fill_a(layer, ct, message_half(layer, LEFT))
        if layer == 0:
            pl.semaphore_wait(barrier, NP - 1 + B - 1 + NX - 1)
        first_a(layer)
        fill_b(layer, cnt, message_half(layer, RIGHT))
        first_b(layer)
        if layer == 0:
            totals = jnp.sum(cnt[...].astype(F32), axis=1, keepdims=True).astype(BF)
            line = lax.rem(iota((S, H), 0), PR)
            spreaded = jnp.where(line == iota((S, H), 1), totals.astype(F32), 0.0).astype(BF)
            pick = jnp.where(iota((NP, S), 1) // PR == iota((NP, S), 0), 1.0, 0.0).astype(BF)
            xs[...] = dot(pick, spreaded).reshape(NP, 1, H)
            scatter(xs, xr, TOT, p, plane_peer, NP)
            m2[...] = pair_permutation(NP)
            sel_n[...] = jnp.where(iota((R, S), 0) == t_n[...], 1.0, 0.0).astype(BF)
            loads[3].wait()
            loads[4].wait()
            loads[5].wait()
        base[...] = dot(st[layer], ws[layer]) + bu[layer:layer + 1, :]
        second_b(layer)
        second_a(layer)
        if layer == 0:
            arrived(xr, TOT)
            grid = xr[...].reshape(NP, H).astype(BF)
            lane = iota((B, H), 1)
            turned = jnp.zeros((B, H), F32)
            for k in range(2):
                chosen = jnp.where(lane == 2 * iota((B, H), 0) + k, 1.0, 0.0).astype(BF)
                put = iota((NP, H), 1) % BR == 2 * iota((NP, H), 0) + k
                put = jnp.where(put, 1.0, 0.0).astype(BF)
                turned = turned + dot(dot_nt(chosen, grid).astype(BF), put)
            ys[...] = turned.reshape(B, 1, H)
            scatter(ys, yr, TOT + 1, b, column_peer, B)
            selt_n[...] = sel_n[...].T
            to_t_order(selt_n, selt_t, R)
            sel_t[...] = selt_t[...].T
            arrived(yr, TOT + 1)
            per = H // BR
            place_of = iota((1, H), 1) // BR
            parts = []
            for k in range(0, B, per):
                part = yr[k]
                for j in range(1, per):
                    part = jnp.where(place_of == j, yr[k + j], part)
                parts.append(part)
            row = jnp.broadcast_to(jnp.concatenate(parts, axis=1), (16, S)).astype(BF)
            weight = dot_nt(sel_t[...], row)
            inv[...] = 1.0 / jnp.maximum(weight[:, 0:1], 1.0)
            st_t[...] = st[0].T
        else:
            cnt_n[...] = cnt[...].T
            cnt_t[...] = ct[...].T
        left = (dot(sel_n[...], final_a(layer)) * inv[...]).astype(BF)
        nm[layer, :, LEFT] = left
        partial = base[...] + dot(left, wn[layer, LEFT, :])
        right = (dot(sel_t[...], final_b(layer)) * inv[...]).astype(BF)
        nm[layer, :, RIGHT] = right
        activated, steep, scaling = settle(partial + dot(right, wn[layer, RIGHT, :]))
        if layer == 0:
            st[1] = (activated * scaling).astype(BF)
            act[...] = activated
            dsl[...] = steep
            scl[...] = scaling

    for turn, layer in ((2, 1), (3, 0)):
        if layer == 1:
            upward = ups[...].astype(F32)
            states = (activated * scaling).astype(BF)
        else:
            upward, activated, steep, scaling = low[...], act[...], dsl[...], scl[...]
        inner = jnp.mean(upward * activated, axis=-1, keepdims=True)
        slope = (scaling * upward - activated * ((scaling * scaling * scaling) * inner)) * steep
        slope_b = slope.astype(BF)
        fill_a(turn, selt_t, (dot_nt(slope_b, wn[layer, LEFT, :]) * inv[...]).astype(BF))
        first_a(turn)
        fill_b(turn, selt_n, (dot_nt(slope_b, wn[layer, RIGHT, :]) * inv[...]).astype(BF))
        first_b(turn)
        if layer == 1:
            emb[...] = states
        update_grad = jnp.sum(slope, axis=0, keepdims=True)
        if layer == 1:
            first_update = update_grad
            place(groups[0][0], 0, dot_tn(st[1], slope_b))
            place(groups[0][0], 1, dot_tn(nm[1], slope_b))
            reduce_1(0)
        else:
            first_offset = jnp.sum(base[...], axis=0, keepdims=True)
            place(groups[1][0], 0, dot_tn(st[1], pb[...]))
            place(groups[1][0], 1, dot(st_t[...], slope_b))
            place(groups[1][0], 2, dot_tn(nm[0], slope_b))
            place_vectors(groups[1][0], 192, (first_update, first_offset, update_grad))
            reduce_1(1)
            reduce_4(0)
        low[...] = dot_nt(slope_b, ws[layer])
        second_b(turn)
        reduce_2(0 if layer == 1 else 1)
        second_a(turn)
        if layer == 1:
            reduce_3(0)
        else:
            reduce_3(1)
            reduce_5(0)
        for half, incoming, counts in ((LEFT, final_a, cnt_n), (RIGHT, final_b, cnt_t)):
            pre_slope = dot(counts[...], incoming(turn)) * dpre[layer, :, half]
            pre_b = pre_slope.astype(BF)
            base[:, half] = pre_slope
            pb[:, half] = pre_b
            if layer == 1:
                low[...] += dot_nt(pre_b, wm[1, :, half])
            else:
                place_half(groups[2][0], 0, half.start // H, dot(st_t[...], pre_b))
        if layer == 0:
            place_vectors(groups[2][0], 64, (jnp.sum(base[...], axis=0, keepdims=True),))
            reduce_1(2)
            reduce_4(1)
            ing[...] = low[...] + dot_nt(pb[...], wm[0])
    reduce_2(2)
    reduce_5(1)
    vectors(1, ((gu, 1), (go, 1), (gu, 0)))
    reduce_3(2)
    result(0, ((gs, 1), (gn, 1)))
    reduce_4(2)
    result(1, ((gm, 1), (gs, 0), (gn, 0)))
    vectors(2, ((go, 0),))
    reduce_5(2)
    result(2, ((gm, 0),))

    for i in range(4):
        await_bytes(sa.at[i, pl.ds(0, B - 1)], ssem.at[4 * i])
        await_bytes(sb.at[i, pl.ds(0, NP - 1)], ssem.at[4 * i + 1])
        await_bytes(mb.at[i, pl.ds(0, B - 1)], ssem.at[4 * i + 2])
        await_bytes(ma.at[i, pl.ds(0, NP - 1)], ssem.at[4 * i + 3])
    await_bytes(xs.at[pl.ds(0, NP - 1)], ssem.at[TOT])
    await_bytes(ys.at[pl.ds(0, B - 1)], ssem.at[TOT + 1])
    for g, bufs in enumerate(groups):
        for stage, (k, n) in enumerate(((1, GROUP), (3, NY), (5, NZ), (7, NY), (8, GROUP))):
            await_bytes(bufs[k].at[pl.ds(0, n - 1)], ssem.at[RED + 5 * g + stage])


def hand_on(*refs):
    n = len(refs) // 2
    for k in range(n):
        refs[n + k][...] = refs[k][...]


def body(NW, NZ, features, upstream, visit_counts, target_rows, wm, bm, ws, wn, bu):
    R = features.shape[0]
    S = visit_counts.shape[0]
    NP, B, NY = NW // NC, NC * NZ, NW // GROUP

    def sum_buffers(matrices, extra):
        rows = 64 * matrices
        piece = rows // NY + extra // 2
        return [
            pltpu.VMEM((GROUP, rows + extra, H), BF),
            pltpu.VMEM((GROUP, rows + extra, H), BF),
            pltpu.VMEM((NY, piece, H), BF),
            pltpu.VMEM((NY, piece, H), BF),
            pltpu.VMEM((piece, H), BF),
            pltpu.VMEM((NZ, piece, H), BF),
            pltpu.VMEM((piece, H), BF),
            pltpu.VMEM((NY, piece, H), BF),
            pltpu.VMEM((GROUP, rows, H), BF),
        ]

    column = pltpu.VMEM((4, B, 2 * NP, H), BF)
    plane = pltpu.VMEM((4, NP, 2 * B, H), BF)
    scratch = [
        pltpu.VMEM((R, F), BF), pltpu.VMEM((R, F), BF), pltpu.VMEM((S, R), BF),
        pltpu.VMEM((2, F, F), BF), pltpu.VMEM((2, F, F), BF), pltpu.VMEM((2, F, F), BF),
        pltpu.VMEM((S, R), BF), pltpu.VMEM((R, S), BF), pltpu.VMEM((R, S), BF),
        pltpu.VMEM((R, S), BF), pltpu.VMEM((R, S), BF),
        pltpu.VMEM((S, R), BF), pltpu.VMEM((S, R), BF),
        pltpu.VMEM((16 * B, 16 * B), BF), pltpu.VMEM((16 * NP, 16 * NP), BF),
        pltpu.VMEM((2, R, F), F32), pltpu.VMEM((R, F), F32), pltpu.VMEM((R, F), F32), pltpu.VMEM((R, 1), F32),
        pltpu.VMEM((2, R, F), BF), pltpu.VMEM((F, R), BF), pltpu.VMEM((2, R, F), BF), pltpu.VMEM((R, F), BF),
        pltpu.VMEM((R, F), F32), pltpu.VMEM((R, F), F32), pltpu.VMEM((R, 1), F32),
        column, column, plane, plane, plane, plane, column, column,
        pltpu.VMEM((NP, 1, H), F32), pltpu.VMEM((NP, 1, H), F32),
        pltpu.VMEM((B, 1, H), F32), pltpu.VMEM((B, 1, H), F32),
    ] + sum_buffers(MATRICES[0], 0) + sum_buffers(MATRICES[1], 16) + sum_buffers(MATRICES[2], 16) + [
        pltpu.SemaphoreType.DMA((6,)), pltpu.SemaphoreType.DMA((33,)), pltpu.SemaphoreType.DMA((33,)),
    ]
    vmem = pl.BlockSpec(memory_space=pltpu.VMEM)
    square = jax.ShapeDtypeStruct((2, F, F), F32)
    line = jax.ShapeDtypeStruct((2, F), F32)
    shapes = (
        jax.ShapeDtypeStruct((R, F), BF), jax.ShapeDtypeStruct((R, F), F32),
        square, line, square, square, line,
    )
    anywhere = pl.BlockSpec(memory_space=pl.ANY)
    outs = pl.pallas_call(
        functools.partial(kernel, NW, NZ, R),
        out_shape=shapes,
        in_specs=[anywhere, anywhere, anywhere, vmem, anywhere, vmem, anywhere, anywhere, vmem],
        out_specs=[vmem] * 7,
        scratch_shapes=scratch,
        compiler_params=pltpu.CompilerParams(
            collective_id=0, has_side_effects=True, vmem_limit_bytes=58 * 2**20),
        cost_estimate=pl.CostEstimate(flops=12 * 2**30, bytes_accessed=2**23, transcendentals=2**20),
    )(features, upstream, visit_counts, target_rows, wm, bm, ws, wn, bu)
    return pl.pallas_call(
        hand_on,
        out_shape=shapes,
        in_specs=[vmem] * len(shapes),
        out_specs=[vmem] * len(shapes),
        compiler_params=pltpu.CompilerParams(vmem_limit_bytes=16 * 2**20),
        cost_estimate=pl.CostEstimate(flops=0, bytes_accessed=2**22, transcendentals=0),
    )(*outs)


def solution(mesh):
    split = P(("wide", "narrow"), None)
    in_specs = (split, split, split, split, P(), P(), P(), P(), P())
    out_specs = (split, split, P(), P(), P(), P(), P())
    run = functools.partial(body, mesh.shape["wide"], mesh.shape["narrow"])
    return jax.shard_map(run, mesh=mesh, in_specs=in_specs, out_specs=out_specs, check_vma=False)
```

```python
import functools

import jax
import jax.numpy as jnp
from jax import lax
from jax.experimental import pallas as pl
from jax.experimental.pallas import tpu as pltpu
from jax.sharding import PartitionSpec as P

F = 256
H = 128
NX = 4
NC = 2
GROUP = NX * NC
EPS = 1e-05
MATRICES = (2, 3, 1)
BF = jnp.bfloat16
F32 = jnp.float32
MESH = pl.DeviceIdType.MESH


def sigmoid(v):
    return 1.0 / (1.0 + jnp.exp(-v))


def dot(a, b):
    return jnp.dot(a, b, preferred_element_type=F32)


def dot_nt(a, b):
    return lax.dot_general(a, b, (((1,), (1,)), ((), ())), preferred_element_type=F32)


def dot_tn(a, b):
    return lax.dot_general(a, b, (((0,), (0,)), ((), ())), preferred_element_type=F32)


def iota(shape, dim):
    return lax.broadcasted_iota(jnp.int32, shape, dim)


def pair_permutation(blocks):
    n = 16 * blocks
    out = iota((n, n), 0)
    source = ((out // 2) % 8) * (2 * blocks) + (out // 16) * 2 + out % 2
    return jnp.where(iota((n, n), 1) == source, 1.0, 0.0).astype(BF)


def alternate(t, n):
    s = (t + 1) // 2
    return lax.rem(s + (1 - lax.rem(t, 2)) * (n - 2 * s), n)


def kernel(
    NW, NZ, R,
    feat_in, ups_in, cnt_in, t_n, wm_in, bm, ws_in, wn_in, bu,
    emb, ing, gm, go, gs, gn, gu,
    feat, ups, cnt, wm, ws, wn,
    ct, cnt_n, cnt_t, sel_n, sel_t, selt_n, selt_t, m1, m2,
    dpre, act, dsl, scl, st, st_t, nm, pb, base, low, inv,
    sa, za, ma, xa, sb, xb, mb, zb,
    xs, xr, ys, yr,
    *rest,
):
    NP = NW // NC
    NY = NP // NX
    B = NC * NZ
    PR, BR = 2 * B, 2 * NP
    S = NP * PR
    wide = lax.axis_index("wide")
    z = lax.axis_index("narrow")
    p, c = wide // NC, lax.rem(wide, NC)
    y, x = p // NX, lax.rem(p, NX)
    q = lax.rem(wide, GROUP)
    b = c * NZ + z

    def plane_peer(d):
        dy = alternate(d // NX, NY)
        yy, xx = lax.rem(y + dy, NY), lax.rem(x + lax.rem(d, NX), NX)
        pp = yy * NX + xx
        return pp, (pp * NC + c, z)

    def column_peer(j):
        dz = alternate(j // 2, NZ)
        cc, zz = lax.rem(c + lax.rem(j, 2), NC), lax.rem(z + dz, NZ)
        return cc * NZ + zz, (p * NC + cc, zz)

    def group_peer(j):
        qq = lax.rem(q + j, GROUP)
        return qq, (y * GROUP + qq, z)

    def row_peer(j):
        yy = lax.rem(y + j, NY)
        return yy, (yy * GROUP + q, z)

    def ring_peer(j):
        zz = lax.rem(z + j, NZ)
        return zz, (wide, zz)

    def send(src, dst, slot, target):
        pltpu.make_async_remote_copy(
            src_ref=src, dst_ref=dst, send_sem=ssem.at[slot], recv_sem=rsem.at[slot],
            device_id=target, device_id_type=MESH,
        ).start()

    def scatter(src, dst, slot, mine, peer, n):
        def step(i, _):
            theirs, target = peer(n - i)
            send(src.at[theirs], dst.at[mine], slot, target)
            return _
        lax.fori_loop(1, n, step, 0)
        dst[pl.ds(mine, 1)] = src[pl.ds(mine, 1)]

    def spread_out(src, dst, slot, mine, peer, n):
        def step(i, _):
            send(src, dst.at[mine], slot, peer(n - i)[1])
            return _
        lax.fori_loop(1, n, step, 0)
        dst[pl.ds(mine, 1)] = src[...][None]

    def await_bytes(ref, sem):
        pltpu.make_async_copy(ref, ref, sem).wait()

    def arrived(dst, slot):
        await_bytes(dst.at[pl.ds(0, dst.shape[0] - 1)], rsem.at[slot])

    groups, (lsem, ssem, rsem) = (rest[:9], rest[9:18], rest[18:27]), rest[27:]
    loads = [
        pltpu.make_async_copy(src, dst, lsem.at[k])
        for k, (src, dst) in enumerate((
            (cnt_in, cnt), (feat_in, feat), (wm_in, wm), (ws_in, ws), (wn_in, wn), (ups_in, ups)))
    ]
    for load in loads:
        load.start()

    barrier = pltpu.get_barrier_semaphore()

    def greet(peer, first, last):
        def step(i, _):
            pl.semaphore_signal(barrier, inc=1, device_id=peer(i)[1], device_id_type=MESH)
            return _
        lax.fori_loop(first, last, step, 0)

    greet(plane_peer, 1, NP)
    greet(column_peer, 1, B)
    greet(lambda i: (i, ((y * NX + lax.rem(x + i, NX)) * NC + (1 - c), z)), 1, NX)

    def to_t_order(src, dst, width):
        for o in range(NP // 8):
            got = dot(m1[...], src[o * 8 * PR:(o + 1) * 8 * PR, :]).astype(BF)
            got = got.reshape(B, 16, width)
            for i in range(B):
                dst[i * BR + o * 16:i * BR + (o + 1) * 16, :] = got[i]

    def shuffle_b(i):
        for o in range(NP // 8):
            got = dot(m1[...], xb[i, o * 8:(o + 1) * 8].reshape(8 * PR, H)).astype(BF)
            mb[i, :, o * 16:(o + 1) * 16, :] = got.reshape(B, 16, H)

    def shuffle_a(i):
        for o in range(B // 8):
            got = dot(m2[...], za[i, o * 8:(o + 1) * 8].reshape(8 * BR, H)).astype(BF)
            ma[i, :, o * 16:(o + 1) * 16, :] = got.reshape(NP, 16, H)

    def fill_a(i, left, right):
        n = max(1, B // 6)
        rows = S // n
        for k in range(n):
            got = dot(left[k * rows:(k + 1) * rows, :], right).astype(BF)
            sa[i, k * (B // n):(k + 1) * (B // n)] = got.reshape(B // n, BR, H)

    def fill_b(i, left, right):
        n = NP // 8
        rows = S // n
        for k in range(n):
            got = dot(left[k * rows:(k + 1) * rows, :], right).astype(BF)
            sb[i, k * 8:(k + 1) * 8] = got.reshape(8, PR, H)

    def first_a(i):
        scatter(sa.at[i], za.at[i], 4 * i, b, column_peer, B)

    def first_b(i):
        scatter(sb.at[i], xb.at[i], 4 * i + 1, p, plane_peer, NP)

    def second_b(i):
        arrived(xb.at[i], 4 * i + 1)
        shuffle_b(i)
        scatter(mb.at[i], zb.at[i], 4 * i + 2, b, column_peer, B)

    def second_a(i):
        arrived(za.at[i], 4 * i)
        shuffle_a(i)
        scatter(ma.at[i], xa.at[i], 4 * i + 3, p, plane_peer, NP)

    def final_a(i):
        arrived(xa.at[i], 4 * i + 3)
        return xa[i].reshape(S, H)

    def final_b(i):
        arrived(zb.at[i], 4 * i + 2)
        return zb[i].reshape(S, H)

    def place_half(buf, matrix, h, value):
        g = value.astype(BF)
        for k in range(GROUP):
            buf[k, matrix * 64 + h * 32:matrix * 64 + (h + 1) * 32, :] = g[k * 32:(k + 1) * 32]

    def place(buf, matrix, value):
        for h in range(2):
            place_half(buf, matrix, h, value[:, h * H:(h + 1) * H])

    def place_vectors(buf, rows, vectors):
        tile = jnp.zeros((16, H), F32)
        line = iota((16, H), 0)
        for v, vec in enumerate(vectors):
            for h in range(2):
                tile = jnp.where(line == 2 * v + h, vec[:, h * H:(h + 1) * H], tile)
        for k in range(GROUP):
            buf[k, rows:rows + 16, :] = tile.astype(BF)

    def reduce_1(g):
        scatter(groups[g][0], groups[g][1], RED + 5 * g, q, group_peer, GROUP)

    def extra(g):
        return groups[g][0].shape[1] - 64 * MATRICES[g]

    def reduce_2(g):
        r, a = groups[g][1], groups[g][2]
        arrived(r, RED + 5 * g)
        rows, piece = 64 * MATRICES[g], 64 * MATRICES[g] // NY
        total = r[0].astype(F32)
        for k in range(1, GROUP):
            total = total + r[k].astype(F32)
        for k in range(NY):
            part = total[k * piece:(k + 1) * piece]
            if extra(g):
                part = jnp.concatenate([part, total[rows:rows + 8]], axis=0)
            a[k] = part.astype(BF)
        scatter(a, groups[g][3], RED + 5 * g + 1, y, row_peer, NY)

    def reduce_3(g):
        r, s = groups[g][3], groups[g][4]
        arrived(r, RED + 5 * g + 1)
        total = r[0].astype(F32)
        for k in range(1, NY):
            total = total + r[k].astype(F32)
        s[...] = total.astype(BF)
        spread_out(s, groups[g][5], RED + 5 * g + 2, z, ring_peer, NZ)

    def reduce_4(g):
        r, s = groups[g][5], groups[g][6]
        arrived(r, RED + 5 * g + 2)
        total = r[0].astype(F32)
        for k in range(1, NZ):
            total = total + r[k].astype(F32)
        s[...] = total.astype(BF)
        spread_out(s, groups[g][7], RED + 5 * g + 3, y, row_peer, NY)

    def reduce_5(g):
        r, out = groups[g][7], groups[g][8]
        arrived(r, RED + 5 * g + 3)
        piece = 64 * MATRICES[g] // NY
        chunk = jnp.concatenate([r[k].astype(F32)[:piece] for k in range(NY)], axis=0)
        out[pl.ds(q, 1)] = chunk.astype(BF)[None]

        def step(i, _):
            send(out.at[q], out.at[q], RED + 5 * g + 4, group_peer(GROUP - i)[1])
            return _
        lax.fori_loop(1, GROUP, step, 0)

    def result(g, targets):
        out = groups[g][8]
        arrived(out, RED + 5 * g + 4)
        for m, (ref, layer) in enumerate(targets):
            for k in range(GROUP):
                for h in range(2):
                    got = out[k, m * 64 + h * 32:m * 64 + (h + 1) * 32, :].astype(F32)
                    ref[layer, k * 32:(k + 1) * 32, h * H:(h + 1) * H] = got

    def vectors(g, targets):
        s = groups[g][6]
        tile = s[s.shape[0] - 16:, :].astype(F32)[8:]
        for v, (ref, layer) in enumerate(targets):
            for h in range(2):
                ref[layer:layer + 1, h * H:(h + 1) * H] = tile[2 * v + h:2 * v + h + 1, :]

    TOT, RED = 16, 18

    def message_half(layer, half):
        value = dot(st[layer], wm[layer, :, half]) + bm[layer:layer + 1, half]
        sigma = sigmoid(value)
        dpre[layer, :, half] = sigma * (1.0 + value * (1.0 - sigma))
        return (value * sigma).astype(BF)

    def settle(value):
        sigma = sigmoid(value)
        activated = value * sigma
        scaling = lax.rsqrt(jnp.mean(activated * activated, axis=-1, keepdims=True) + EPS)
        return activated, sigma * (1.0 + value * (1.0 - sigma)), scaling

    LEFT, RIGHT = slice(0, H), slice(H, F)

    m1[...] = pair_permutation(B)
    loads[0].wait()
    to_t_order(cnt, ct, R)
    loads[1].wait()
    loads[2].wait()
    st[0] = feat[...]
    for layer in range(2):
        fill_a(layer, ct, message_half(layer, LEFT))
        if layer == 0:
            pl.semaphore_wait(barrier, NP - 1 + B - 1 + NX - 1)
        first_a(layer)
        fill_b(layer, cnt, message_half(layer, RIGHT))
        first_b(layer)
        if layer == 0:
            totals = jnp.sum(cnt[...].astype(F32), axis=1, keepdims=True).astype(BF)
            line = lax.rem(iota((S, H), 0), PR)
            spreaded = jnp.where(line == iota((S, H), 1), totals.astype(F32), 0.0).astype(BF)
            pick = jnp.where(iota((NP, S), 1) // PR == iota((NP, S), 0), 1.0, 0.0).astype(BF)
            xs[...] = dot(pick, spreaded).reshape(NP, 1, H)
            scatter(xs, xr, TOT, p, plane_peer, NP)
            m2[...] = pair_permutation(NP)
            sel_n[...] = jnp.where(iota((R, S), 0) == t_n[...], 1.0, 0.0).astype(BF)
            loads[3].wait()
            loads[4].wait()
            loads[5].wait()
        base[...] = dot(st[layer], ws[layer]) + bu[layer:layer + 1, :]
        second_b(layer)
        second_a(layer)
        if layer == 0:
            arrived(xr, TOT)
            grid = xr[...].reshape(NP, H).astype(BF)
            lane = iota((B, H), 1)
            turned = jnp.zeros((B, H), F32)
            for k in range(2):
                chosen = jnp.where(lane == 2 * iota((B, H), 0) + k, 1.0, 0.0).astype(BF)
                put = iota((NP, H), 1) % BR == 2 * iota((NP, H), 0) + k
                put = jnp.where(put, 1.0, 0.0).astype(BF)
                turned = turned + dot(dot_nt(chosen, grid).astype(BF), put)
            ys[...] = turned.reshape(B, 1, H)
            scatter(ys, yr, TOT + 1, b, column_peer, B)
            selt_n[...] = sel_n[...].T
            to_t_order(selt_n, selt_t, R)
            sel_t[...] = selt_t[...].T
            arrived(yr, TOT + 1)
            per = H // BR
            place_of = iota((1, H), 1) // BR
            parts = []
            for k in range(0, B, per):
                part = yr[k]
                for j in range(1, per):
                    part = jnp.where(place_of == j, yr[k + j], part)
                parts.append(part)
            row = jnp.broadcast_to(jnp.concatenate(parts, axis=1), (16, S)).astype(BF)
            weight = dot_nt(sel_t[...], row)
            inv[...] = 1.0 / jnp.maximum(weight[:, 0:1], 1.0)
            st_t[...] = st[0].T
        else:
            cnt_n[...] = cnt[...].T
            cnt_t[...] = ct[...].T
        left = (dot(sel_n[...], final_a(layer)) * inv[...]).astype(BF)
        nm[layer, :, LEFT] = left
        partial = base[...] + dot(left, wn[layer, LEFT, :])
        right = (dot(sel_t[...], final_b(layer)) * inv[...]).astype(BF)
        nm[layer, :, RIGHT] = right
        activated, steep, scaling = settle(partial + dot(right, wn[layer, RIGHT, :]))
        if layer == 0:
            st[1] = (activated * scaling).astype(BF)
            act[...] = activated
            dsl[...] = steep
            scl[...] = scaling

    for turn, layer in ((2, 1), (3, 0)):
        if layer == 1:
            upward = ups[...].astype(F32)
            states = (activated * scaling).astype(BF)
        else:
            upward, activated, steep, scaling = low[...], act[...], dsl[...], scl[...]
        inner = jnp.mean(upward * activated, axis=-1, keepdims=True)
        slope = (scaling * upward - activated * ((scaling * scaling * scaling) * inner)) * steep
        slope_b = slope.astype(BF)
        fill_a(turn, selt_t, (dot_nt(slope_b, wn[layer, LEFT, :]) * inv[...]).astype(BF))
        first_a(turn)
        fill_b(turn, selt_n, (dot_nt(slope_b, wn[layer, RIGHT, :]) * inv[...]).astype(BF))
        first_b(turn)
        if layer == 1:
            emb[...] = states
        update_grad = jnp.sum(slope, axis=0, keepdims=True)
        if layer == 1:
            first_update = update_grad
            place(groups[0][0], 0, dot_tn(st[1], slope_b))
            place(groups[0][0], 1, dot_tn(nm[1], slope_b))
            reduce_1(0)
        else:
            first_offset = jnp.sum(base[...], axis=0, keepdims=True)
            place(groups[1][0], 0, dot_tn(st[1], pb[...]))
            place(groups[1][0], 1, dot(st_t[...], slope_b))
            place(groups[1][0], 2, dot_tn(nm[0], slope_b))
            place_vectors(groups[1][0], 192, (first_update, first_offset, update_grad))
            reduce_1(1)
            reduce_4(0)
        low[...] = dot_nt(slope_b, ws[layer])
        second_b(turn)
        reduce_2(0 if layer == 1 else 1)
        second_a(turn)
        if layer == 1:
            reduce_3(0)
        else:
            reduce_3(1)
            reduce_5(0)
        for half, incoming, counts in ((LEFT, final_a, cnt_n), (RIGHT, final_b, cnt_t)):
            pre_slope = dot(counts[...], incoming(turn)) * dpre[layer, :, half]
            pre_b = pre_slope.astype(BF)
            base[:, half] = pre_slope
            pb[:, half] = pre_b
            if layer == 1:
                low[...] += dot_nt(pre_b, wm[1, :, half])
            else:
                place_half(groups[2][0], 0, half.start // H, dot(st_t[...], pre_b))
        if layer == 0:
            place_vectors(groups[2][0], 64, (jnp.sum(base[...], axis=0, keepdims=True),))
            reduce_1(2)
            reduce_4(1)
            ing[...] = low[...] + dot_nt(pb[...], wm[0])
    reduce_2(2)
    reduce_5(1)
    vectors(1, ((gu, 1), (go, 1), (gu, 0)))
    reduce_3(2)
    result(0, ((gs, 1), (gn, 1)))
    reduce_4(2)
    vectors(2, ((go, 0),))
    reduce_5(2)
    result(1, ((gm, 1), (gs, 0), (gn, 0)))
    result(2, ((gm, 0),))

    for i in range(4):
        await_bytes(sa.at[i, pl.ds(0, B - 1)], ssem.at[4 * i])
        await_bytes(sb.at[i, pl.ds(0, NP - 1)], ssem.at[4 * i + 1])
        await_bytes(mb.at[i, pl.ds(0, B - 1)], ssem.at[4 * i + 2])
        await_bytes(ma.at[i, pl.ds(0, NP - 1)], ssem.at[4 * i + 3])
    await_bytes(xs.at[pl.ds(0, NP - 1)], ssem.at[TOT])
    await_bytes(ys.at[pl.ds(0, B - 1)], ssem.at[TOT + 1])
    for g, bufs in enumerate(groups):
        for stage, (k, n) in enumerate(((1, GROUP), (3, NY), (5, NZ), (7, NY), (8, GROUP))):
            await_bytes(bufs[k].at[pl.ds(0, n - 1)], ssem.at[RED + 5 * g + stage])


def hand_on(*refs):
    n = (len(refs) - 2) // 3
    sources, outs, held, (in_sem, out_sem) = refs[:n], refs[n:2 * n], refs[2 * n:3 * n], refs[3 * n:]
    reads = [pltpu.make_async_copy(sources[k], held[k], in_sem.at[k]) for k in range(n)]
    writes = [pltpu.make_async_copy(held[k], outs[k], out_sem.at[k]) for k in range(n)]
    for read in reads:
        read.start()
    for read, write in zip(reads, writes):
        read.wait()
        write.start()
    for write in writes:
        write.wait()


def body(NW, NZ, features, upstream, visit_counts, target_rows, wm, bm, ws, wn, bu):
    R = features.shape[0]
    S = visit_counts.shape[0]
    NP, B, NY = NW // NC, NC * NZ, NW // GROUP

    def sum_buffers(matrices, extra):
        rows = 64 * matrices
        piece = rows // NY + extra // 2
        return [
            pltpu.VMEM((GROUP, rows + extra, H), BF),
            pltpu.VMEM((GROUP, rows + extra, H), BF),
            pltpu.VMEM((NY, piece, H), BF),
            pltpu.VMEM((NY, piece, H), BF),
            pltpu.VMEM((piece, H), BF),
            pltpu.VMEM((NZ, piece, H), BF),
            pltpu.VMEM((piece, H), BF),
            pltpu.VMEM((NY, piece, H), BF),
            pltpu.VMEM((GROUP, rows, H), BF),
        ]

    column = pltpu.VMEM((4, B, 2 * NP, H), BF)
    plane = pltpu.VMEM((4, NP, 2 * B, H), BF)
    scratch = [
        pltpu.VMEM((R, F), BF), pltpu.VMEM((R, F), BF), pltpu.VMEM((S, R), BF),
        pltpu.VMEM((2, F, F), BF), pltpu.VMEM((2, F, F), BF), pltpu.VMEM((2, F, F), BF),
        pltpu.VMEM((S, R), BF), pltpu.VMEM((R, S), BF), pltpu.VMEM((R, S), BF),
        pltpu.VMEM((R, S), BF), pltpu.VMEM((R, S), BF),
        pltpu.VMEM((S, R), BF), pltpu.VMEM((S, R), BF),
        pltpu.VMEM((16 * B, 16 * B), BF), pltpu.VMEM((16 * NP, 16 * NP), BF),
        pltpu.VMEM((2, R, F), F32), pltpu.VMEM((R, F), F32), pltpu.VMEM((R, F), F32), pltpu.VMEM((R, 1), F32),
        pltpu.VMEM((2, R, F), BF), pltpu.VMEM((F, R), BF), pltpu.VMEM((2, R, F), BF), pltpu.VMEM((R, F), BF),
        pltpu.VMEM((R, F), F32), pltpu.VMEM((R, F), F32), pltpu.VMEM((R, 1), F32),
        column, column, plane, plane, plane, plane, column, column,
        pltpu.VMEM((NP, 1, H), F32), pltpu.VMEM((NP, 1, H), F32),
        pltpu.VMEM((B, 1, H), F32), pltpu.VMEM((B, 1, H), F32),
    ] + sum_buffers(MATRICES[0], 0) + sum_buffers(MATRICES[1], 16) + sum_buffers(MATRICES[2], 16) + [
        pltpu.SemaphoreType.DMA((6,)), pltpu.SemaphoreType.DMA((33,)), pltpu.SemaphoreType.DMA((33,)),
    ]
    vmem = pl.BlockSpec(memory_space=pltpu.VMEM)
    square = jax.ShapeDtypeStruct((2, F, F), F32)
    line = jax.ShapeDtypeStruct((2, F), F32)
    shapes = (
        jax.ShapeDtypeStruct((R, F), BF), jax.ShapeDtypeStruct((R, F), F32),
        square, line, square, square, line,
    )
    anywhere = pl.BlockSpec(memory_space=pl.ANY)
    outs = pl.pallas_call(
        functools.partial(kernel, NW, NZ, R),
        out_shape=shapes,
        in_specs=[anywhere, anywhere, anywhere, vmem, anywhere, vmem, anywhere, anywhere, vmem],
        out_specs=[vmem] * 7,
        scratch_shapes=scratch,
        compiler_params=pltpu.CompilerParams(
            collective_id=0, has_side_effects=True, vmem_limit_bytes=58 * 2**20),
        cost_estimate=pl.CostEstimate(flops=12 * 2**30, bytes_accessed=2**23, transcendentals=2**20),
    )(features, upstream, visit_counts, target_rows, wm, bm, ws, wn, bu)
    return pl.pallas_call(
        hand_on,
        out_shape=shapes,
        in_specs=[anywhere] * len(shapes),
        out_specs=[anywhere] * len(shapes),
        scratch_shapes=[pltpu.VMEM(shape.shape, shape.dtype) for shape in shapes] + [
            pltpu.SemaphoreType.DMA((len(shapes),)), pltpu.SemaphoreType.DMA((len(shapes),)),
        ],
        compiler_params=pltpu.CompilerParams(vmem_limit_bytes=60 * 2**20),
        cost_estimate=pl.CostEstimate(flops=0, bytes_accessed=2**22, transcendentals=0),
    )(*outs)


def solution(mesh):
    split = P(("wide", "narrow"), None)
    in_specs = (split, split, split, split, P(), P(), P(), P(), P())
    out_specs = (split, split, P(), P(), P(), P(), P())
    run = functools.partial(body, mesh.shape["wide"], mesh.shape["narrow"])
    return jax.shard_map(run, mesh=mesh, in_specs=in_specs, out_specs=out_specs, check_vma=False)
```
